256 devices in a mesh: seq: 32 (over y, x, core), head: 8 (over z).
Axes of the slice: x: 4, y: 4, z: 8, core: 2. Of those that a mesh axis runs over, the one named last changes fastest.
Arguments:
- queries: bfloat16 [32, 128, 16384], P('seq', None, 'head'), parts along dimension 2
- cache_keys: bfloat16 [262144, 1024], P('seq', 'head'), parts along dimension 1
- cache_values: bfloat16 [262144, 1024], P('seq', 'head'), parts along dimension 1
- lengths: int32 [32], replicated, may hold values from 1 to 8192, as said below
- span_owner: int32 [1], replicated, may hold values from 0 to 31
Outputs:
- attended: bfloat16 [32, 128, 16384], P('seq', None, 'head'), parts along dimension 2
The draws below stay inside these ranges and needn't reach their ends.
There are 8 independent parts, one for each index of `head`. The reference program is written for one: setup_inputs(seed, part) draws one part's arguments, and reference() takes and returns one part's arrays. A program takes and returns all parts, laid end to end along the dimension named above; an argument that names none is the same for every part. Nothing has to cross between parts.
Inputs may be any that keep to these rules, and one draw needn't show every extreme that they name: `lengths`: every shard but the last holds 8192 valid positions.
All inputs are finite; a program needn't handle non-finite values.
Results may differ from the reference program's by a relative error of at most 0.0019.
Values may be sent and summed in bfloat16 or wider, within the bound.
No kernel may reach another device: no remote copies, remote signals or barrier semaphores. Data moves between devices by JAX's collectives and lax.ppermute only.
A program may use at most 128 MiB of HBM per device.

```python
import jax
import jax.numpy as jnp
from jax import lax

DH = 128
QH = 16
SPAN = 128
S_DEV = 8192
SHARDS = 32
KEYS_ALL = 262144


def base_keys(key, low_scale, high_scale):
    noise = jax.random.normal(jax.random.fold_in(key, 101), (KEYS_ALL, DH), jnp.float32)
    spread = jax.random.uniform(jax.random.fold_in(key, 102), (KEYS_ALL, 1), jnp.float32, low_scale, high_scale)
    return noise * spread


def draw_cache_keys(key, part):
    planted = base_keys(key, 1.0, 1.0)
    return planted.astype(jnp.bfloat16)


def draw_queries(key, part):
    key = jax.random.fold_in(key, 2)
    result = jax.random.normal(key, (SHARDS, SPAN, QH * DH), jnp.float32)
    return result.astype(jnp.bfloat16)


def draw_cache_values(key, part):
    key = jax.random.fold_in(key, 3)
    noise = 0.5 * jax.random.normal(jax.random.fold_in(key, 1), (SHARDS, S_DEV, DH), jnp.float32)
    offsets = jax.random.uniform(jax.random.fold_in(key, 2), (SHARDS, 1, DH), jnp.float32, -3.0, 3.0)
    return (noise + offsets).reshape(KEYS_ALL, DH).astype(jnp.bfloat16)


def draw_lengths(key, part):
    key = jax.random.fold_in(key, 4)
    last_len = jax.random.randint(key, (), 1, S_DEV + 1)
    return jnp.full((SHARDS,), S_DEV, jnp.int32).at[SHARDS - 1].set(last_len)


def setup_inputs(seed: int = 0, part: int = 0) -> dict:
    keys = jax.random.split(jax.random.key(seed), 6)
    part_splits = jax.random.split(jax.random.fold_in(keys[5], part), 6)
    return {
        "queries": draw_queries(jax.random.fold_in(jax.random.fold_in(keys[5], part), 71), part),
        "cache_keys": draw_cache_keys(jax.random.fold_in(jax.random.fold_in(keys[5], part), 71), part),
        "cache_values": draw_cache_values(jax.random.fold_in(jax.random.fold_in(keys[5], part), 71), part),
        "lengths": draw_lengths(jax.random.fold_in(keys[5], 71), part),
        "span_owner": jax.random.randint(keys[4], (1,), 0, SHARDS).astype(jnp.int32),
    }


def shard_partial(query_rows, shard_keys, shard_values, valid_len):
    score_scale = 1.0 / jnp.sqrt(jnp.float32(DH))
    scores = lax.dot_general(query_rows, shard_keys, (((1,), (1,)), ((), ())), preferred_element_type=jnp.float32) * score_scale
    columns = jnp.arange(shard_keys.shape[0], dtype=jnp.int32)
    scores = jnp.where(columns[None, :] < valid_len, scores, -jnp.inf)
    row_max = lax.optimization_barrier(jnp.max(scores, axis=1))
    weights = jnp.exp(scores - row_max[:, None])
    row_sum = lax.optimization_barrier(jnp.sum(weights, axis=1))
    weighted = jnp.dot(weights.astype(jnp.bfloat16), shard_values, preferred_element_type=jnp.float32)
    return (row_max, row_sum, weighted)

def reference(queries, cache_keys, cache_values, lengths, span_owner):
    owner_index = span_owner[0].astype(jnp.int32)
    block = lax.dynamic_index_in_dim(queries, owner_index, 0, keepdims=False)
    query_rows = block.reshape(SPAN * QH, DH)
    keys_split = cache_keys.reshape(SHARDS, S_DEV, DH)
    values_split = cache_values.reshape(SHARDS, S_DEV, DH)

    def one_shard(items):
        return shard_partial(query_rows, items[0], items[1], items[2])
    row_max, row_sum, weighted = lax.map(one_shard, (keys_split, values_split, lengths))
    top = lax.optimization_barrier(jnp.max(row_max, axis=0))
    factor = jnp.exp(row_max - top[None, :])
    denom = lax.optimization_barrier(jnp.sum(factor * row_sum, axis=0))
    numer = lax.optimization_barrier(jnp.sum(factor[:, :, None] * weighted, axis=0))
    result = (numer / denom[:, None]).astype(jnp.bfloat16).reshape(1, SPAN, QH * DH)
    full = jnp.zeros((SHARDS, SPAN, QH * DH), jnp.bfloat16)
    return lax.dynamic_update_slice(full, result, (owner_index, jnp.int32(0), jnp.int32(0)))
```

```python
import functools
import math

import jax
import jax.numpy as jnp
from jax import lax
from jax.experimental import pallas as pl
from jax.experimental.pallas import tpu as pltpu
from jax.sharding import PartitionSpec as P

AXIS = "seq"
CHIPS = 16
HEAD = 128
PIECE = 64
TAIL = 8
ROWS = PIECE + TAIL
VROWS = HEAD + 16
BLOCK = 256
STEP = 512
BF16 = jnp.bfloat16
F32 = jnp.float32
LOG2_SCALE = math.log2(math.e) / math.sqrt(HEAD)
NT = (((1,), (1,)), ((), ()))

SWAP = [(i, i ^ 1) for i in range(2 * CHIPS)]
PLANE = [[2 * chip + core for chip in range(CHIPS)] for core in range(2)]


def vmem(limit):
    return pltpu.CompilerParams(vmem_limit_bytes=limit << 20)


def exchange(pieces):
    return lax.all_to_all(pieces, AXIS, 0, 0, axis_index_groups=PLANE, tiled=True)


def values_kernel(len_ref, v_ref, o_ref):
    size = v_ref.shape[0]
    lanes = lax.broadcasted_iota(jnp.int32, (HEAD, HEAD), 1)
    eye = (lanes == lax.broadcasted_iota(jnp.int32, (HEAD, HEAD), 0)).astype(BF16)
    turned = lax.dot_general(eye, v_ref[...], NT, preferred_element_type=F32)
    column = pl.program_id(0) * size + lax.broadcasted_iota(jnp.int32, (1, size), 1)
    valid = column < len_ref[0]
    o_ref[:HEAD, :] = jnp.where(valid, turned, 0.0).astype(BF16)
    o_ref[HEAD:, :] = jnp.broadcast_to(jnp.where(valid, 1.0, 0.0), (16, size)).astype(BF16)


def turned_values(valid_len, values):
    keys = values.shape[0]
    size = 2048
    return pl.pallas_call(
        values_kernel,
        out_shape=jax.ShapeDtypeStruct((VROWS, keys), BF16),
        grid_spec=pltpu.PrefetchScalarGridSpec(
            num_scalar_prefetch=1,
            grid=(keys // size,),
            in_specs=[pl.BlockSpec((size, HEAD), lambda i, n: (i, 0))],
            out_specs=pl.BlockSpec((VROWS, size), lambda i, n: (0, i)),
        ),
        compiler_params=vmem(16),
        name="turn_values",
    )(valid_len, values)


def attention_kernel(len_ref, q_ref, k_ref, v_ref, o_ref, acc_ref):
    q = q_ref[...]

    def write(out, sums, top):
        row = lax.broadcasted_iota(jnp.int32, (TAIL, HEAD), 0)
        for head in range(BLOCK // HEAD):
            lanes = slice(head * HEAD, (head + 1) * HEAD)
            tail = jnp.where(row < TAIL // 2, sums[:, lanes], top[:, lanes])
            for part in range(2):
                o_ref[2 * head + part, :PIECE, :] = out[part * PIECE : (part + 1) * PIECE, lanes]
                o_ref[2 * head + part, PIECE:, :] = tail

    scores = lax.dot_general(k_ref[...], q, NT, preferred_element_type=F32)
    weights = jnp.exp2(scores * LOG2_SCALE).astype(BF16)
    total = jnp.dot(v_ref[...], weights, preferred_element_type=F32)
    sums = total[HEAD : HEAD + 1, :]
    write(total[:HEAD], sums, jnp.zeros_like(sums))
    low = jnp.min(sums)
    high = jnp.max(sums)
    largest = jnp.max(jnp.abs(total[:HEAD]))
    fine = (low >= 1.0) & (high <= 2.0**20) & (largest < 3e38)

    @pl.when(jnp.logical_not(fine))
    def _():
        acc_ref[...] = jnp.zeros_like(acc_ref)

        def body(i, top):
            start = pl.multiple_of(i * STEP, STEP)
            s = lax.dot_general(k_ref[pl.ds(start, STEP), :], q, NT, preferred_element_type=F32)
            row = start + lax.broadcasted_iota(jnp.int32, (STEP, 1), 0)
            s = jnp.where(row < len_ref[0], s * LOG2_SCALE, -jnp.inf)
            new_top = jnp.maximum(top, jnp.max(s, axis=0, keepdims=True))
            w = jnp.exp2(s - new_top).astype(BF16)
            part = jnp.dot(v_ref[:, pl.ds(start, STEP)], w, preferred_element_type=F32)
            acc_ref[...] = acc_ref[...] * jnp.exp2(top - new_top) + part
            return new_top

        start_top = jnp.full((1, BLOCK), -jnp.inf, F32)
        top = lax.fori_loop(0, k_ref.shape[0] // STEP, body, start_top)
        write(acc_ref[:HEAD, :], acc_ref[HEAD : HEAD + 1, :], top)


def attention(valid_len, rows, keys, values):
    blocks = rows.shape[0] // BLOCK
    pieces = 2 * BLOCK // HEAD
    return pl.pallas_call(
        attention_kernel,
        out_shape=jax.ShapeDtypeStruct((blocks * pieces, ROWS, HEAD), F32),
        grid_spec=pltpu.PrefetchScalarGridSpec(
            num_scalar_prefetch=1,
            grid=(blocks,),
            in_specs=[
                pl.BlockSpec((BLOCK, HEAD), lambda i, n: (i, 0)),
                pl.BlockSpec(keys.shape, lambda i, n: (0, 0)),
                pl.BlockSpec(values.shape, lambda i, n: (0, 0)),
            ],
            out_specs=pl.BlockSpec((pieces, ROWS, HEAD), lambda i, n: (i, 0, 0)),
            scratch_shapes=[pltpu.VMEM((VROWS, BLOCK), F32)],
        ),
        compiler_params=vmem(44),
        cost_estimate=pl.CostEstimate(
            flops=4 * rows.shape[0] * keys.shape[0] * HEAD,
            bytes_accessed=4 * keys.shape[0] * HEAD,
            transcendentals=rows.shape[0] * keys.shape[0],
        ),
        name="attention",
    )(valid_len, rows, keys, values)


def merge_kernel(a_ref, b_ref, o_ref):
    top_a = a_ref[:, ROWS - 1 :, :]
    top_b = b_ref[:, ROWS - 1 :, :]
    top = jnp.maximum(top_a, top_b)
    left = jnp.exp2(top_a - top)
    right = jnp.exp2(top_b - top)
    o_ref[:, :PIECE, :] = left * a_ref[:, :PIECE, :] + right * b_ref[:, :PIECE, :]
    sums = left * a_ref[:, PIECE : PIECE + 1, :] + right * b_ref[:, PIECE : PIECE + 1, :]
    row = lax.broadcasted_iota(jnp.int32, (1, TAIL, HEAD), 1)
    o_ref[:, PIECE:, :] = jnp.where(row < TAIL // 2, sums, top)


def merge(a, b):
    return pl.pallas_call(
        merge_kernel,
        out_shape=jax.ShapeDtypeStruct(a.shape, F32),
        compiler_params=vmem(16),
        name="merge",
    )(a, b)


def finish_kernel(r_ref, o_ref):
    tops = r_ref[:, ROWS - 1 :, :]
    scale = jnp.exp2(tops - jnp.max(tops, axis=0, keepdims=True))
    denom = jnp.sum(scale * r_ref[:, PIECE : PIECE + 1, :], axis=0)
    numer = jnp.sum(scale * r_ref[:, :PIECE, :], axis=0)
    result = (numer / denom).astype(BF16)
    o_ref[...] = jnp.broadcast_to(result[None], o_ref.shape)


def finish(received):
    return pl.pallas_call(
        finish_kernel,
        out_shape=jax.ShapeDtypeStruct((CHIPS, PIECE, HEAD), BF16),
        compiler_params=vmem(16),
        name="finish",
    )(received)


def place_kernel(flags_ref, a_ref, b_ref, o_ref):
    half = o_ref.shape[1] // 2

    @pl.when(flags_ref[0] == 0)
    def _():
        o_ref[...] = jnp.zeros_like(o_ref)

    def put(first, second):
        for i, ref in enumerate((first, second)):
            for h in range(half // HEAD):
                block = ref[h * HEAD : (h + 1) * HEAD, :]
                o_ref[:, i * half + h * HEAD : i * half + (h + 1) * HEAD] = block.T

    @pl.when((flags_ref[0] == 1) & (flags_ref[1] == 0))
    def _():
        put(a_ref, b_ref)

    @pl.when((flags_ref[0] == 1) & (flags_ref[1] == 1))
    def _():
        put(b_ref, a_ref)


def place(flags, own, other):
    return pl.pallas_call(
        place_kernel,
        out_shape=jax.ShapeDtypeStruct((HEAD, 2 * own.shape[0]), BF16),
        in_specs=[
            pl.BlockSpec(memory_space=pltpu.SMEM),
            pl.BlockSpec(memory_space=pltpu.VMEM),
            pl.BlockSpec(memory_space=pltpu.VMEM),
        ],
        compiler_params=vmem(16),
        name="place",
    )(flags, own, other)


def per_device(queries, cache_keys, cache_values, lengths, span_owner):
    me = lax.axis_index(AXIS)
    core = me % 2
    owner = span_owner[0]
    valid_len = lax.dynamic_slice(lengths, (me,), (1,))
    block = queries[0]
    span, width = block.shape
    half = width // 2

    def pieces(index):
        part = lax.dynamic_slice(block, (0, index * half), (span, half))
        part = part.reshape(span, half // HEAD, HEAD).transpose(1, 0, 2)
        return part.reshape(CHIPS, PIECE, HEAD)

    values = turned_values(valid_len, cache_values)
    received = lax.ppermute(pieces(1 - core), AXIS, SWAP)
    mine = jnp.where(owner % 2 == core, pieces(core), received)
    piece = lax.dynamic_index_in_dim(exchange(mine), owner // 2, 0, False)
    own = exchange(jnp.broadcast_to(piece[None], mine.shape))
    other = lax.ppermute(own, AXIS, SWAP)

    attend = functools.partial(attention, valid_len, keys=cache_keys, values=values)
    part_other = attend(other.reshape(half, HEAD))
    part_peer = lax.ppermute(part_other, AXIS, SWAP)
    part_own = attend(own.reshape(half, HEAD))
    result = finish(exchange(merge(part_own, part_peer)))
    result = exchange(result)
    result_other = lax.ppermute(result, AXIS, SWAP)
    flags = jnp.stack([(me == owner).astype(jnp.int32), core])
    out = place(flags, result.reshape(half, HEAD), result_other.reshape(half, HEAD))
    return out[None]


def solution(mesh):
    return jax.shard_map(
        per_device,
        mesh=mesh,
        in_specs=(P("seq", None, "head"), P("seq", "head"), P("seq", "head"), P(), P()),
        out_specs=P("seq", None, "head"),
        check_vma=False,
    )
```

```python
import functools
import math

import jax
import jax.numpy as jnp
from jax import lax
from jax.experimental import pallas as pl
from jax.experimental.pallas import tpu as pltpu
from jax.sharding import PartitionSpec as P

AXIS = "seq"
CHIPS = 16
HEAD = 128
PIECE = 64
TAIL = 8
ROWS = PIECE + TAIL
VROWS = HEAD + 16
BLOCK = 512
STEP = 512
BF16 = jnp.bfloat16
F32 = jnp.float32
LOG2_SCALE = math.log2(math.e) / math.sqrt(HEAD)
NT = (((1,), (1,)), ((), ()))

SWAP = [(i, i ^ 1) for i in range(2 * CHIPS)]
PLANE = [[2 * chip + core for chip in range(CHIPS)] for core in range(2)]


def vmem(limit):
    return pltpu.CompilerParams(vmem_limit_bytes=limit << 20)


def exchange(pieces):
    return lax.all_to_all(pieces, AXIS, 0, 0, axis_index_groups=PLANE, tiled=True)


def prepare_kernel(len_ref, k_ref, v_ref, kept_ref, turned_ref):
    size = v_ref.shape[0]
    kept_ref[...] = k_ref[...]
    lanes = lax.broadcasted_iota(jnp.int32, (HEAD, HEAD), 1)
    eye = (lanes == lax.broadcasted_iota(jnp.int32, (HEAD, HEAD), 0)).astype(BF16)
    turned = lax.dot_general(eye, v_ref[...], NT, preferred_element_type=F32)
    column = pl.program_id(0) * size + lax.broadcasted_iota(jnp.int32, (1, size), 1)
    valid = column < len_ref[lax.axis_index(AXIS)]
    turned_ref[:HEAD, :] = jnp.where(valid, turned, 0.0).astype(BF16)
    turned_ref[HEAD:, :] = jnp.broadcast_to(jnp.where(valid, 1.0, 0.0), (16, size)).astype(BF16)


def prepare(lengths, keys, values):
    count = keys.shape[0]
    size = 2048
    rows = pl.BlockSpec((size, HEAD), lambda i, n: (i, 0))
    return pl.pallas_call(
        prepare_kernel,
        out_shape=(
            jax.ShapeDtypeStruct(keys.shape, BF16),
            jax.ShapeDtypeStruct((VROWS, count), BF16),
        ),
        grid_spec=pltpu.PrefetchScalarGridSpec(
            num_scalar_prefetch=1,
            grid=(count // size,),
            in_specs=[rows, rows],
            out_specs=(rows, pl.BlockSpec((VROWS, size), lambda i, n: (0, i))),
        ),
        compiler_params=vmem(16),
        cost_estimate=pl.CostEstimate(
            flops=4 * count * HEAD * HEAD, bytes_accessed=8 * count * HEAD, transcendentals=0
        ),
        name="prepare",
    )(lengths, keys, values)


def attention_kernel(q_ref, k_ref, v_ref, o_ref, acc_ref):
    q = q_ref[...]

    def write(out, sums, top):
        row = lax.broadcasted_iota(jnp.int32, (TAIL, HEAD), 0)
        for head in range(BLOCK // HEAD):
            lanes = slice(head * HEAD, (head + 1) * HEAD)
            tail = jnp.where(row < TAIL // 2, sums[:, lanes], top[:, lanes])
            for part in range(2):
                o_ref[2 * head + part, :PIECE, :] = out[part * PIECE : (part + 1) * PIECE, lanes]
                o_ref[2 * head + part, PIECE:, :] = tail

    scores = lax.dot_general(k_ref[...], q, NT, preferred_element_type=F32)
    weights = jnp.exp2(scores * LOG2_SCALE).astype(BF16)
    total = jnp.dot(v_ref[...], weights, preferred_element_type=F32)
    sums = total[HEAD : HEAD + 1, :]
    write(total[:HEAD], sums, jnp.zeros_like(sums))
    good = (sums >= 1.0) & (sums <= 2.0**20)
    bad = jnp.max(jnp.where(jnp.abs(total[:HEAD]) < 3e38, 0.0, 1.0), axis=0, keepdims=True)
    fine = jnp.max(jnp.where(good, bad, 1.0)) < 0.5

    @pl.when(jnp.logical_not(fine))
    def _():
        acc_ref[...] = jnp.zeros_like(acc_ref)
        valid_len = jnp.sum(v_ref[HEAD : HEAD + 1, :].astype(F32)).astype(jnp.int32)

        def body(i, top):
            start = pl.multiple_of(i * STEP, STEP)
            s = lax.dot_general(k_ref[pl.ds(start, STEP), :], q, NT, preferred_element_type=F32)
            row = start + lax.broadcasted_iota(jnp.int32, (STEP, 1), 0)
            s = jnp.where(row < valid_len, s * LOG2_SCALE, -jnp.inf)
            new_top = jnp.maximum(top, jnp.max(s, axis=0, keepdims=True))
            w = jnp.exp2(s - new_top).astype(BF16)
            part = jnp.dot(v_ref[:, pl.ds(start, STEP)], w, preferred_element_type=F32)
            acc_ref[...] = acc_ref[...] * jnp.exp2(top - new_top) + part
            return new_top

        start_top = jnp.full((1, BLOCK), -jnp.inf, F32)
        top = lax.fori_loop(0, k_ref.shape[0] // STEP, body, start_top)
        write(acc_ref[:HEAD, :], acc_ref[HEAD : HEAD + 1, :], top)


def attention(rows, keys, values, first, blocks):
    pieces = 2 * BLOCK // HEAD
    return pl.pallas_call(
        attention_kernel,
        out_shape=jax.ShapeDtypeStruct((blocks * pieces, ROWS, HEAD), F32),
        grid=(blocks,),
        in_specs=[
            pl.BlockSpec((BLOCK, HEAD), lambda i: (i + first, 0)),
            pl.BlockSpec(keys.shape, lambda i: (0, 0)),
            pl.BlockSpec(values.shape, lambda i: (0, 0)),
        ],
        out_specs=pl.BlockSpec((pieces, ROWS, HEAD), lambda i: (i, 0, 0)),
        scratch_shapes=[pltpu.VMEM((VROWS, BLOCK), F32)],
        compiler_params=vmem(44),
        cost_estimate=pl.CostEstimate(
            flops=4 * blocks * BLOCK * keys.shape[0] * HEAD,
            bytes_accessed=4 * keys.shape[0] * HEAD,
            transcendentals=blocks * BLOCK * keys.shape[0],
        ),
        name="attention",
    )(rows, keys, values)


def merge_kernel(a_ref, b_ref, peer_ref, o_ref):
    first = a_ref.shape[0]

    def put(mine, start):
        stop = start + mine.shape[0]
        top_a = mine[:, ROWS - 1 :, :]
        top_b = peer_ref[start:stop, ROWS - 1 :, :]
        top = jnp.maximum(top_a, top_b)
        left = jnp.exp2(top_a - top)
        right = jnp.exp2(top_b - top)
        o_ref[start:stop, :PIECE, :] = (
            left * mine[:, :PIECE, :] + right * peer_ref[start:stop, :PIECE, :]
        )
        sums = left * mine[:, PIECE : PIECE + 1, :]
        sums += right * peer_ref[start:stop, PIECE : PIECE + 1, :]
        row = lax.broadcasted_iota(jnp.int32, (1, TAIL, HEAD), 1)
        o_ref[start:stop, PIECE:, :] = jnp.where(row < TAIL // 2, sums, top)

    put(a_ref, 0)
    put(b_ref, first)


def merge(a, b, peer):
    return pl.pallas_call(
        merge_kernel,
        out_shape=jax.ShapeDtypeStruct(peer.shape, F32),
        compiler_params=vmem(16),
        name="merge",
    )(a, b, peer)


def split_kernel(q_ref, keep_ref, send_ref):
    half = q_ref.shape[1] // 2

    def put(ref, start):
        for h in range(half // HEAD):
            block = q_ref[:, start + h * HEAD : start + (h + 1) * HEAD]
            ref[2 * h] = block[:PIECE]
            ref[2 * h + 1] = block[PIECE:]

    core = lax.axis_index(AXIS) % 2

    @pl.when(core == 0)
    def _():
        put(keep_ref, 0)
        put(send_ref, half)

    @pl.when(core == 1)
    def _():
        put(keep_ref, half)
        put(send_ref, 0)


def split(block):
    shape = jax.ShapeDtypeStruct((CHIPS, PIECE, HEAD), BF16)
    return pl.pallas_call(
        split_kernel,
        out_shape=(shape, shape),
        compiler_params=vmem(16),
        name="split",
    )(block)


def choose_kernel(owner_ref, a_ref, b_ref, o_ref):
    mine = owner_ref[0] % 2 == lax.axis_index(AXIS) % 2

    @pl.when(mine)
    def _():
        o_ref[...] = a_ref[...]

    @pl.when(jnp.logical_not(mine))
    def _():
        o_ref[...] = b_ref[...]


def choose(owner, a, b):
    return pl.pallas_call(
        choose_kernel,
        out_shape=jax.ShapeDtypeStruct(a.shape, a.dtype),
        in_specs=[
            pl.BlockSpec(memory_space=pltpu.SMEM),
            pl.BlockSpec(memory_space=pltpu.VMEM),
            pl.BlockSpec(memory_space=pltpu.VMEM),
        ],
        compiler_params=vmem(16),
        name="choose",
    )(owner, a, b)


def finish_kernel(r_ref, o_ref):
    tops = r_ref[:, ROWS - 1 :, :]
    scale = jnp.exp2(tops - jnp.max(tops, axis=0, keepdims=True))
    denom = jnp.sum(scale * r_ref[:, PIECE : PIECE + 1, :], axis=0)
    numer = jnp.sum(scale * r_ref[:, :PIECE, :], axis=0)
    result = (numer / denom).astype(BF16)
    o_ref[...] = jnp.broadcast_to(result[None], o_ref.shape)


def finish(received):
    return pl.pallas_call(
        finish_kernel,
        out_shape=jax.ShapeDtypeStruct((CHIPS, PIECE, HEAD), BF16),
        compiler_params=vmem(16),
        name="finish",
    )(received)


def place_kernel(owner_ref, a_ref, b_ref, o_ref):
    half = o_ref.shape[1] // 2

    me = lax.axis_index(AXIS)
    wanted = me == owner_ref[0]

    @pl.when(jnp.logical_not(wanted))
    def _():
        o_ref[...] = jnp.zeros_like(o_ref)

    def put(first, second):
        for i, ref in enumerate((first, second)):
            for h in range(half // HEAD):
                block = ref[h * HEAD : (h + 1) * HEAD, :]
                o_ref[:, i * half + h * HEAD : i * half + (h + 1) * HEAD] = block.T

    @pl.when(wanted & (me % 2 == 0))
    def _():
        put(a_ref, b_ref)

    @pl.when(wanted & (me % 2 == 1))
    def _():
        put(b_ref, a_ref)


def place(owner, own, other):
    return pl.pallas_call(
        place_kernel,
        out_shape=jax.ShapeDtypeStruct((HEAD, 2 * own.shape[0]), BF16),
        in_specs=[
            pl.BlockSpec(memory_space=pltpu.SMEM),
            pl.BlockSpec(memory_space=pltpu.VMEM),
            pl.BlockSpec(memory_space=pltpu.VMEM),
        ],
        compiler_params=vmem(16),
        name="place",
    )(owner, own, other)


def per_device(queries, cache_keys, cache_values, lengths, span_owner):
    block = queries[0]
    half = block.shape[1] // 2

    keep, send = split(block)
    received = lax.ppermute(send, AXIS, SWAP)
    mine = choose(span_owner, keep, received)
    lengths, mine = lax.optimization_barrier((lengths, mine))
    keys, values = prepare(lengths, cache_keys, cache_values)
    piece = lax.dynamic_index_in_dim(exchange(mine), span_owner[0] // 2, 0, False)
    piece, keys, values = lax.optimization_barrier((piece, keys, values))
    own = exchange(jnp.broadcast_to(piece[None], mine.shape))
    other = lax.ppermute(own, AXIS, SWAP).reshape(half, HEAD)
    own = own.reshape(half, HEAD)

    attend = functools.partial(attention, keys=keys, values=values)
    blocks = half // BLOCK
    part_a = attend(own, first=0, blocks=blocks // 2)
    part_a, other = lax.optimization_barrier((part_a, other))
    part_other = attend(other, first=0, blocks=blocks)
    part_peer = lax.ppermute(part_other, AXIS, SWAP)
    own, _ = lax.optimization_barrier((own, part_other))
    part_b = attend(own, first=blocks // 2, blocks=blocks - blocks // 2)
    result = finish(exchange(merge(part_a, part_b, part_peer)))
    result = exchange(result)
    result_other = lax.ppermute(result, AXIS, SWAP)
    out = place(span_owner, result.reshape(half, HEAD), result_other.reshape(half, HEAD))
    return out[None]


def solution(mesh):
    return jax.shard_map(
        per_device,
        mesh=mesh,
        in_specs=(P("seq", None, "head"), P("seq", "head"), P("seq", "head"), P(), P()),
        out_specs=P("seq", None, "head"),
        check_vma=False,
    )
```

```python
import functools
import math

import jax
import jax.numpy as jnp
from jax import lax
from jax.experimental import pallas as pl
from jax.experimental.pallas import tpu as pltpu
from jax.sharding import PartitionSpec as P

AXIS = "seq"
CHIPS = 16
HEAD = 128
PIECE = 64
TAIL = 8
ROWS = PIECE + TAIL
VROWS = HEAD + 16
COLUMNS = 4
BLOCK = 512
PIECES = 2 * BLOCK // HEAD
STEP = 512
CHUNKS = 4
BF16 = jnp.bfloat16
F32 = jnp.float32
LOG2_SCALE = math.log2(math.e) / math.sqrt(HEAD)
NT = (((1,), (1,)), ((), ()))

SWAP = [(i, i ^ 1) for i in range(2 * CHIPS)]
PLANE = [[2 * chip + core for chip in range(CHIPS)] for core in range(2)]


def device(y, x, core):
    return (y * COLUMNS + x % COLUMNS) * 2 + core


def partner(y, x, core):
    return device(y, x + (1 if (x + core) % 2 == 0 else -1), core)


EVERY = [(y, x, core) for y in range(COLUMNS) for x in range(COLUMNS) for core in range(2)]
PAIR = [(device(*place), partner(*place)) for place in EVERY]
CROSS = [(device(y, x, 1 - core), partner(y, x, core)) for y, x, core in EVERY]
TEAMS = [
    [device(y, x, core) for y in range(COLUMNS) for x in (side, side + 2)]
    for core in range(2)
    for side in range(2)
]


def member(chip):
    y, x = divmod(chip, COLUMNS)
    return x % 2, 2 * y + x // 2


def vmem(limit):
    return pltpu.CompilerParams(vmem_limit_bytes=limit << 20)


def exchange(pieces, groups):
    return lax.all_to_all(pieces, AXIS, 0, 0, axis_index_groups=groups, tiled=True)


def values_kernel(len_ref, v_ref, o_ref):
    size = v_ref.shape[0]
    lanes = lax.broadcasted_iota(jnp.int32, (HEAD, HEAD), 1)
    eye = (lanes == lax.broadcasted_iota(jnp.int32, (HEAD, HEAD), 0)).astype(BF16)
    turned = lax.dot_general(eye, v_ref[...], NT, preferred_element_type=F32)
    column = pl.program_id(0) * size + lax.broadcasted_iota(jnp.int32, (1, size), 1)
    valid = column < len_ref[lax.axis_index(AXIS)]
    o_ref[:HEAD, :] = jnp.where(valid, turned, 0.0).astype(BF16)
    o_ref[HEAD:, :] = jnp.broadcast_to(jnp.where(valid, 1.0, 0.0), (16, size)).astype(BF16)


def turned_values(lengths, values):
    keys = values.shape[0]
    size = 2048
    return pl.pallas_call(
        values_kernel,
        out_shape=jax.ShapeDtypeStruct((VROWS, keys), BF16),
        grid_spec=pltpu.PrefetchScalarGridSpec(
            num_scalar_prefetch=1,
            grid=(keys // size,),
            in_specs=[pl.BlockSpec((size, HEAD), lambda i, n: (i, 0))],
            out_specs=pl.BlockSpec((VROWS, size), lambda i, n: (0, i)),
        ),
        compiler_params=vmem(16),
        cost_estimate=pl.CostEstimate(
            flops=4 * keys * HEAD * HEAD, bytes_accessed=5 * keys * HEAD, transcendentals=0
        ),
        name="turn_values",
    )(lengths, values)


def write_block(o_ref, out, sums, top):
    row = lax.broadcasted_iota(jnp.int32, (TAIL, HEAD), 0)
    for head in range(BLOCK // HEAD):
        lanes = slice(head * HEAD, (head + 1) * HEAD)
        tail = jnp.where(row < TAIL // 2, sums[:, lanes], top[:, lanes])
        for part in range(2):
            o_ref[2 * head + part, :PIECE, :] = out[part * PIECE : (part + 1) * PIECE, lanes]
            o_ref[2 * head + part, PIECE:, :] = tail


def weigh(q, keys, values):
    scores = lax.dot_general(keys, q, NT, preferred_element_type=F32)
    weights = jnp.exp2(scores * LOG2_SCALE).astype(BF16)
    return jnp.dot(values, weights, preferred_element_type=F32)


def settle(total, q, k_ref, v_ref, o_ref, acc_ref):
    sums = total[HEAD : HEAD + 1, :]
    write_block(o_ref, total[:HEAD], sums, jnp.zeros_like(sums))
    good = (sums >= 1.0) & (sums <= 2.0**20)
    bad = jnp.max(jnp.where(jnp.abs(total[:HEAD]) < 3e38, 0.0, 1.0), axis=0, keepdims=True)
    fine = jnp.max(jnp.where(good, bad, 1.0)) < 0.5

    @pl.when(jnp.logical_not(fine))
    def _():
        acc_ref[...] = jnp.zeros_like(acc_ref)
        valid_len = jnp.sum(v_ref[HEAD : HEAD + 1, :].astype(F32)).astype(jnp.int32)

        def body(i, top):
            at = pl.multiple_of(i * STEP, STEP)
            s = lax.dot_general(k_ref[pl.ds(at, STEP), :], q, NT, preferred_element_type=F32)
            row = at + lax.broadcasted_iota(jnp.int32, (STEP, 1), 0)
            s = jnp.where(row < valid_len, s * LOG2_SCALE, -jnp.inf)
            new_top = jnp.maximum(top, jnp.max(s, axis=0, keepdims=True))
            w = jnp.exp2(s - new_top).astype(BF16)
            part = jnp.dot(v_ref[:, pl.ds(at, STEP)], w, preferred_element_type=F32)
            acc_ref[...] = acc_ref[...] * jnp.exp2(top - new_top) + part
            return new_top

        start_top = jnp.full((1, BLOCK), -jnp.inf, F32)
        top = lax.fori_loop(0, k_ref.shape[0] // STEP, body, start_top)
        write_block(o_ref, acc_ref[:HEAD, :], acc_ref[HEAD : HEAD + 1, :], top)


def attention_kernel(q_ref, k_ref, v_ref, o_ref, acc_ref):
    q = q_ref[...]
    settle(weigh(q, k_ref[...], v_ref[...]), q, k_ref, v_ref, o_ref, acc_ref)


def first_attention_kernel(q_ref, k_ref, v_ref, o_ref, kept_ref, acc_ref, sems):
    size = k_ref.shape[0] // CHUNKS
    spans = [slice(i * size, (i + 1) * size) for i in range(CHUNKS)]
    copies = [
        pltpu.make_async_copy(k_ref.at[span], kept_ref.at[span], sems.at[i])
        for i, span in enumerate(spans)
    ]
    for copy in copies:
        copy.start()
    q = q_ref[...]
    total = None
    for copy, span in zip(copies, spans):
        copy.wait()
        part = weigh(q, kept_ref[span, :], v_ref[:, span])
        total = part if total is None else total + part
    settle(total, q, kept_ref, v_ref, o_ref, acc_ref)


def attention(rows, keys, values, first=False):
    vmem_spec = pl.BlockSpec(memory_space=pltpu.VMEM)
    out = jax.ShapeDtypeStruct((PIECES, ROWS, HEAD), F32)
    scratch = [pltpu.VMEM((VROWS, BLOCK), F32)]
    return pl.pallas_call(
        first_attention_kernel if first else attention_kernel,
        out_shape=(out, jax.ShapeDtypeStruct(keys.shape, BF16)) if first else out,
        in_specs=[vmem_spec, pl.BlockSpec(memory_space=pltpu.HBM) if first else vmem_spec, vmem_spec],
        out_specs=(vmem_spec, vmem_spec) if first else vmem_spec,
        scratch_shapes=scratch + ([pltpu.SemaphoreType.DMA((CHUNKS,))] if first else []),
        compiler_params=vmem(44),
        cost_estimate=pl.CostEstimate(
            flops=BLOCK * keys.size // 2, bytes_accessed=keys.size, transcendentals=0
        ),
        name="attention",
    )(rows.reshape(BLOCK, HEAD), keys, values)


def merge_kernel(*refs):
    parts, o_ref = refs[:-1], refs[-1]
    tops = [ref[:, ROWS - 1 :, :] for ref in parts]
    top = functools.reduce(jnp.maximum, tops)
    scales = [jnp.exp2(t - top) for t in tops]
    sums = sum(w * ref[:, PIECE : PIECE + 1, :] for w, ref in zip(scales, parts))
    row = lax.broadcasted_iota(jnp.int32, (1, TAIL, HEAD), 1)
    o_ref[:, :PIECE, :] = sum(w * ref[:, :PIECE, :] for w, ref in zip(scales, parts))
    o_ref[:, PIECE:, :] = jnp.where(row < TAIL // 2, sums, top)


def merge(*parts):
    return pl.pallas_call(
        merge_kernel,
        out_shape=jax.ShapeDtypeStruct(parts[0].shape, F32),
        compiler_params=vmem(16),
        name="merge",
    )(*parts)


def split_kernel(q_ref, keep_ref, send_ref):
    half = q_ref.shape[1] // 2

    def put(ref, start):
        for chip in range(CHIPS):
            side, place = member(chip)
            head, part = divmod((1 - side) * PIECES + place, 2)
            column = start + head * HEAD
            ref[chip] = q_ref[part * PIECE : (part + 1) * PIECE, column : column + HEAD]

    core = lax.axis_index(AXIS) % 2

    @pl.when(core == 0)
    def _():
        put(keep_ref, 0)
        put(send_ref, half)

    @pl.when(core == 1)
    def _():
        put(keep_ref, half)
        put(send_ref, 0)


def split(block):
    shape = jax.ShapeDtypeStruct((CHIPS, PIECE, HEAD), BF16)
    return pl.pallas_call(
        split_kernel,
        out_shape=(shape, shape),
        compiler_params=vmem(16),
        name="split",
    )(block)


def choose_kernel(owner_ref, a_ref, b_ref, o_ref):
    mine = owner_ref[0] % 2 == lax.axis_index(AXIS) % 2

    @pl.when(mine)
    def _():
        o_ref[...] = a_ref[...]

    @pl.when(jnp.logical_not(mine))
    def _():
        o_ref[...] = b_ref[...]


def choose(owner, a, b):
    return pl.pallas_call(
        choose_kernel,
        out_shape=jax.ShapeDtypeStruct(a.shape, a.dtype),
        in_specs=[
            pl.BlockSpec(memory_space=pltpu.SMEM),
            pl.BlockSpec(memory_space=pltpu.VMEM),
            pl.BlockSpec(memory_space=pltpu.VMEM),
        ],
        compiler_params=vmem(16),
        name="choose",
    )(owner, a, b)


def finish_kernel(r_ref, o_ref):
    tops = r_ref[:, ROWS - 1 :, :]
    scale = jnp.exp2(tops - jnp.max(tops, axis=0, keepdims=True))
    denom = jnp.sum(scale * r_ref[:, PIECE : PIECE + 1, :], axis=0)
    numer = jnp.sum(scale * r_ref[:, :PIECE, :], axis=0)
    result = (numer / denom).astype(BF16)
    o_ref[...] = jnp.broadcast_to(result[None], o_ref.shape)


def finish(received):
    return pl.pallas_call(
        finish_kernel,
        out_shape=jax.ShapeDtypeStruct((CHIPS, PIECE, HEAD), BF16),
        compiler_params=vmem(16),
        name="finish",
    )(received)


def place_kernel(owner_ref, a_ref, b_ref, o_ref):
    half = o_ref.shape[1] // 2

    me = lax.axis_index(AXIS)
    wanted = me == owner_ref[0]

    @pl.when(jnp.logical_not(wanted))
    def _():
        o_ref[...] = jnp.zeros_like(o_ref)

    def put(first, second):
        for i, ref in enumerate((first, second)):
            for chip in range(0, CHIPS):
                side, spot = member(chip)
                if spot % 2 == 0:
                    head = (side * PIECES + spot) // 2
                    block = jnp.concatenate([ref[chip], ref[chip + 2]], axis=0)
                    o_ref[:, i * half + head * HEAD : i * half + (head + 1) * HEAD] = block.T

    @pl.when(wanted & (me % 2 == 0))
    def _():
        put(a_ref, b_ref)

    @pl.when(wanted & (me % 2 == 1))
    def _():
        put(b_ref, a_ref)


def place(owner, own, other):
    return pl.pallas_call(
        place_kernel,
        out_shape=jax.ShapeDtypeStruct((HEAD, 2 * CHIPS * PIECE), BF16),
        in_specs=[
            pl.BlockSpec(memory_space=pltpu.SMEM),
            pl.BlockSpec(memory_space=pltpu.VMEM),
            pl.BlockSpec(memory_space=pltpu.VMEM),
        ],
        compiler_params=vmem(16),
        name="place",
    )(owner, own, other)


def per_device(queries, cache_keys, cache_values, lengths, span_owner):
    keep, send = split(queries[0])
    mine = choose(span_owner, keep, lax.ppermute(send, AXIS, SWAP))
    lengths, mine = lax.optimization_barrier((lengths, mine))
    values = turned_values(lengths, cache_values)
    piece = lax.dynamic_index_in_dim(exchange(mine, PLANE), span_owner[0] // 2, 0, False)
    piece, values = lax.optimization_barrier((piece, values))

    own_away = exchange(jnp.broadcast_to(piece[None], (PIECES, PIECE, HEAD)), TEAMS)
    other_away = lax.ppermute(own_away, AXIS, SWAP)
    own_here = lax.ppermute(own_away, AXIS, PAIR)

    cache_keys = pltpu.with_memory_space_constraint(cache_keys, pltpu.HBM)
    part, keys = attention(own_away, cache_keys, values, first=True)
    part, other_away, own_here, keys = lax.optimization_barrier((part, other_away, own_here, keys))
    here_1 = lax.ppermute(part, AXIS, PAIR)
    other_here = lax.ppermute(own_here, AXIS, SWAP)
    part = attention(other_away, keys, values)
    part, other_here = lax.optimization_barrier((part, other_here))
    here_2 = lax.ppermute(part, AXIS, CROSS)
    part = attention(other_here, keys, values)
    part, own_here = lax.optimization_barrier((part, own_here))
    here_3 = lax.ppermute(part, AXIS, SWAP)
    part = attention(own_here, keys, values)

    received = exchange(merge(part, here_3, merge(here_1, here_2)), TEAMS)
    result = exchange(finish(received), PLANE)
    out = place(span_owner, result, lax.ppermute(result, AXIS, SWAP))
    return out[None]


def solution(mesh):
    return jax.shard_map(
        per_device,
        mesh=mesh,
        in_specs=(P("seq", None, "head"), P("seq", "head"), P("seq", "head"), P(), P()),
        out_specs=P("seq", None, "head"),
        check_vma=False,
    )
```

```python
import functools
import math

import jax
import jax.numpy as jnp
from jax import lax
from jax.experimental import pallas as pl
from jax.experimental.pallas import tpu as pltpu
from jax.sharding import PartitionSpec as P

AXIS = "seq"
CHIPS = 16
HEAD = 128
PIECE = 64
TAIL = 8
ROWS = PIECE + TAIL
VROWS = HEAD + 16
COLUMNS = 4
BLOCK = 512
PIECES = 2 * BLOCK // HEAD
STEP = 512
CHUNK = 2048
BF16 = jnp.bfloat16
F32 = jnp.float32
LOG2_SCALE = math.log2(math.e) / math.sqrt(HEAD)
NT = (((1,), (1,)), ((), ()))

SWAP = [(i, i ^ 1) for i in range(2 * CHIPS)]
PLANE = [[2 * chip + core for chip in range(CHIPS)] for core in range(2)]


def device(y, x, core):
    return (y * COLUMNS + x % COLUMNS) * 2 + core


def partner(y, x, core):
    return device(y, x + (1 if (x + core) % 2 == 0 else -1), core)


EVERY = [(y, x, core) for y in range(COLUMNS) for x in range(COLUMNS) for core in range(2)]
PAIR = [(device(*place), partner(*place)) for place in EVERY]
CROSS = [(device(y, x, 1 - core), partner(y, x, core)) for y, x, core in EVERY]
TEAMS = [
    [device(y, x, core) for y in range(COLUMNS) for x in (side, side + 2)]
    for core in range(2)
    for side in range(2)
]


def member(chip):
    y, x = divmod(chip, COLUMNS)
    return x % 2, 2 * y + x // 2


def vmem(limit):
    return pltpu.CompilerParams(vmem_limit_bytes=limit << 20)


def exchange(pieces, groups):
    return lax.all_to_all(pieces, AXIS, 0, 0, axis_index_groups=groups, tiled=True)


def values_kernel(len_ref, k_ref, v_ref, head_ref, o_ref):
    size = v_ref.shape[0]

    @pl.when(pl.program_id(0) == 0)
    def _():
        head_ref[...] = k_ref[...]

    lanes = lax.broadcasted_iota(jnp.int32, (HEAD, HEAD), 1)
    eye = (lanes == lax.broadcasted_iota(jnp.int32, (HEAD, HEAD), 0)).astype(BF16)
    turned = lax.dot_general(eye, v_ref[...], NT, preferred_element_type=F32)
    column = pl.program_id(0) * size + lax.broadcasted_iota(jnp.int32, (1, size), 1)
    valid = column < len_ref[lax.axis_index(AXIS)]
    o_ref[:HEAD, :] = jnp.where(valid, turned, 0.0).astype(BF16)
    o_ref[HEAD:, :] = jnp.broadcast_to(jnp.where(valid, 1.0, 0.0), (16, size)).astype(BF16)


def turned_values(lengths, keys, values):
    count = values.shape[0]
    head = pl.BlockSpec((CHUNK, HEAD), lambda i, n: (0, 0))
    return pl.pallas_call(
        values_kernel,
        out_shape=(
            jax.ShapeDtypeStruct((CHUNK, HEAD), BF16),
            jax.ShapeDtypeStruct((VROWS, count), BF16),
        ),
        grid_spec=pltpu.PrefetchScalarGridSpec(
            num_scalar_prefetch=1,
            grid=(count // CHUNK,),
            in_specs=[head, pl.BlockSpec((CHUNK, HEAD), lambda i, n: (i, 0))],
            out_specs=(head, pl.BlockSpec((VROWS, CHUNK), lambda i, n: (0, i))),
        ),
        compiler_params=vmem(16),
        cost_estimate=pl.CostEstimate(
            flops=4 * count * HEAD * HEAD, bytes_accessed=5 * count * HEAD, transcendentals=0
        ),
        name="turn_values",
    )(lengths, pltpu.with_memory_space_constraint(keys, pltpu.HBM), values)


def write_block(o_ref, out, sums, top):
    row = lax.broadcasted_iota(jnp.int32, (TAIL, HEAD), 0)
    for head in range(BLOCK // HEAD):
        lanes = slice(head * HEAD, (head + 1) * HEAD)
        tail = jnp.where(row < TAIL // 2, sums[:, lanes], top[:, lanes])
        for part in range(2):
            o_ref[2 * head + part, :PIECE, :] = out[part * PIECE : (part + 1) * PIECE, lanes]
            o_ref[2 * head + part, PIECE:, :] = tail


def weigh(q, keys, values):
    scores = lax.dot_general(keys, q, NT, preferred_element_type=F32)
    weights = jnp.exp2(scores * LOG2_SCALE).astype(BF16)
    return jnp.dot(values, weights, preferred_element_type=F32)


def settle(total, q, k_ref, v_ref, o_ref, acc_ref):
    sums = total[HEAD : HEAD + 1, :]
    write_block(o_ref, total[:HEAD], sums, jnp.zeros_like(sums))
    good = (sums >= 1.0) & (sums <= 2.0**20)
    bad = jnp.max(jnp.where(jnp.abs(total[:HEAD]) < 3e38, 0.0, 1.0), axis=0, keepdims=True)
    fine = jnp.max(jnp.where(good, bad, 1.0)) < 0.5

    @pl.when(jnp.logical_not(fine))
    def _():
        acc_ref[...] = jnp.zeros_like(acc_ref)
        valid_len = jnp.sum(v_ref[HEAD : HEAD + 1, :].astype(F32)).astype(jnp.int32)

        def body(i, top):
            at = pl.multiple_of(i * STEP, STEP)
            s = lax.dot_general(k_ref[pl.ds(at, STEP), :], q, NT, preferred_element_type=F32)
            row = at + lax.broadcasted_iota(jnp.int32, (STEP, 1), 0)
            s = jnp.where(row < valid_len, s * LOG2_SCALE, -jnp.inf)
            new_top = jnp.maximum(top, jnp.max(s, axis=0, keepdims=True))
            w = jnp.exp2(s - new_top).astype(BF16)
            part = jnp.dot(v_ref[:, pl.ds(at, STEP)], w, preferred_element_type=F32)
            acc_ref[...] = acc_ref[...] * jnp.exp2(top - new_top) + part
            return new_top

        start_top = jnp.full((1, BLOCK), -jnp.inf, F32)
        top = lax.fori_loop(0, k_ref.shape[0] // STEP, body, start_top)
        write_block(o_ref, acc_ref[:HEAD, :], acc_ref[HEAD : HEAD + 1, :], top)


def attention_kernel(q_ref, k_ref, v_ref, o_ref, acc_ref):
    q = q_ref[...]
    settle(weigh(q, k_ref[...], v_ref[...]), q, k_ref, v_ref, o_ref, acc_ref)


def first_attention_kernel(q_ref, head_ref, k_ref, v_ref, o_ref, kept_ref, acc_ref, sems):
    spans = [slice(start, start + CHUNK) for start in range(0, k_ref.shape[0], CHUNK)]
    copies = [
        pltpu.make_async_copy(k_ref.at[span] if i else head_ref, kept_ref.at[span], sems.at[i])
        for i, span in enumerate(spans)
    ]
    for copy in copies[1:] + copies[:1]:
        copy.start()
    q = q_ref[...]
    total = weigh(q, head_ref[...], v_ref[:, spans[0]])
    for copy, span in zip(copies[1:], spans[1:]):
        copy.wait()
        total += weigh(q, kept_ref[span, :], v_ref[:, span])
    copies[0].wait()
    settle(total, q, kept_ref, v_ref, o_ref, acc_ref)


def first_attention(rows, head, keys, values):
    vmem_spec = pl.BlockSpec(memory_space=pltpu.VMEM)
    return pl.pallas_call(
        first_attention_kernel,
        out_shape=(
            jax.ShapeDtypeStruct((PIECES, ROWS, HEAD), F32),
            jax.ShapeDtypeStruct(keys.shape, BF16),
        ),
        in_specs=[vmem_spec, vmem_spec, pl.BlockSpec(memory_space=pltpu.HBM), vmem_spec],
        out_specs=(vmem_spec, vmem_spec),
        scratch_shapes=[
            pltpu.VMEM((VROWS, BLOCK), F32),
            pltpu.SemaphoreType.DMA((keys.shape[0] // CHUNK,)),
        ],
        compiler_params=vmem(44),
        cost_estimate=pl.CostEstimate(
            flops=BLOCK * keys.size // 2, bytes_accessed=keys.size, transcendentals=0
        ),
        name="first_attention",
    )(rows.reshape(BLOCK, HEAD), head, pltpu.with_memory_space_constraint(keys, pltpu.HBM), values)


def attention(rows, keys, values):
    vmem_spec = pl.BlockSpec(memory_space=pltpu.VMEM)
    return pl.pallas_call(
        attention_kernel,
        out_shape=jax.ShapeDtypeStruct((PIECES, ROWS, HEAD), F32),
        in_specs=[vmem_spec] * 3,
        out_specs=vmem_spec,
        scratch_shapes=[pltpu.VMEM((VROWS, BLOCK), F32)],
        compiler_params=vmem(44),
        cost_estimate=pl.CostEstimate(
            flops=BLOCK * keys.size // 2, bytes_accessed=keys.size, transcendentals=0
        ),
        name="attention",
    )(rows.reshape(BLOCK, HEAD), keys, values)


def merge_kernel(*refs):
    parts, o_ref = refs[:-1], refs[-1]
    tops = [ref[:, ROWS - 1 :, :] for ref in parts]
    top = functools.reduce(jnp.maximum, tops)
    scales = [jnp.exp2(t - top) for t in tops]
    sums = sum(w * ref[:, PIECE : PIECE + 1, :] for w, ref in zip(scales, parts))
    row = lax.broadcasted_iota(jnp.int32, (1, TAIL, HEAD), 1)
    o_ref[:, :PIECE, :] = sum(w * ref[:, :PIECE, :] for w, ref in zip(scales, parts))
    o_ref[:, PIECE:, :] = jnp.where(row < TAIL // 2, sums, top)


def merge(*parts):
    return pl.pallas_call(
        merge_kernel,
        out_shape=jax.ShapeDtypeStruct(parts[0].shape, F32),
        compiler_params=vmem(16),
        name="merge",
    )(*parts)


def split_kernel(q_ref, keep_ref, send_ref):
    half = q_ref.shape[1] // 2

    def put(ref, start):
        for chip in range(CHIPS):
            side, place = member(chip)
            head, part = divmod((1 - side) * PIECES + place, 2)
            column = start + head * HEAD
            ref[chip] = q_ref[part * PIECE : (part + 1) * PIECE, column : column + HEAD]

    core = lax.axis_index(AXIS) % 2

    @pl.when(core == 0)
    def _():
        put(keep_ref, 0)
        put(send_ref, half)

    @pl.when(core == 1)
    def _():
        put(keep_ref, half)
        put(send_ref, 0)


def split(block):
    shape = jax.ShapeDtypeStruct((CHIPS, PIECE, HEAD), BF16)
    return pl.pallas_call(
        split_kernel,
        out_shape=(shape, shape),
        compiler_params=vmem(16),
        name="split",
    )(block)


def choose_kernel(owner_ref, a_ref, b_ref, o_ref):
    mine = owner_ref[0] % 2 == lax.axis_index(AXIS) % 2

    @pl.when(mine)
    def _():
        o_ref[...] = a_ref[...]

    @pl.when(jnp.logical_not(mine))
    def _():
        o_ref[...] = b_ref[...]


def choose(owner, a, b):
    return pl.pallas_call(
        choose_kernel,
        out_shape=jax.ShapeDtypeStruct(a.shape, a.dtype),
        in_specs=[
            pl.BlockSpec(memory_space=pltpu.SMEM),
            pl.BlockSpec(memory_space=pltpu.VMEM),
            pl.BlockSpec(memory_space=pltpu.VMEM),
        ],
        compiler_params=vmem(16),
        name="choose",
    )(owner, a, b)


def finish_kernel(r_ref, o_ref):
    tops = r_ref[:, ROWS - 1 :, :]
    scale = jnp.exp2(tops - jnp.max(tops, axis=0, keepdims=True))
    denom = jnp.sum(scale * r_ref[:, PIECE : PIECE + 1, :], axis=0)
    numer = jnp.sum(scale * r_ref[:, :PIECE, :], axis=0)
    result = (numer / denom).astype(BF16)
    o_ref[...] = jnp.broadcast_to(result[None], o_ref.shape)


def finish(received):
    return pl.pallas_call(
        finish_kernel,
        out_shape=jax.ShapeDtypeStruct((CHIPS, PIECE, HEAD), BF16),
        compiler_params=vmem(16),
        name="finish",
    )(received)


def place_kernel(owner_ref, a_ref, b_ref, o_ref):
    half = o_ref.shape[1] // 2

    me = lax.axis_index(AXIS)
    wanted = me == owner_ref[0]

    @pl.when(jnp.logical_not(wanted))
    def _():
        o_ref[...] = jnp.zeros_like(o_ref)

    def put(first, second):
        for i, ref in enumerate((first, second)):
            for chip in range(0, CHIPS):
                side, spot = member(chip)
                if spot % 2 == 0:
                    head = (side * PIECES + spot) // 2
                    block = jnp.concatenate([ref[chip], ref[chip + 2]], axis=0)
                    o_ref[:, i * half + head * HEAD : i * half + (head + 1) * HEAD] = block.T

    @pl.when(wanted & (me % 2 == 0))
    def _():
        put(a_ref, b_ref)

    @pl.when(wanted & (me % 2 == 1))
    def _():
        put(b_ref, a_ref)


def place(owner, own, other):
    return pl.pallas_call(
        place_kernel,
        out_shape=jax.ShapeDtypeStruct((HEAD, 2 * CHIPS * PIECE), BF16),
        in_specs=[
            pl.BlockSpec(memory_space=pltpu.SMEM),
            pl.BlockSpec(memory_space=pltpu.VMEM),
            pl.BlockSpec(memory_space=pltpu.VMEM),
        ],
        compiler_params=vmem(16),
        name="place",
    )(owner, own, other)


def per_device(queries, cache_keys, cache_values, lengths, span_owner):
    keep, send = split(queries[0])
    mine = choose(span_owner, keep, lax.ppermute(send, AXIS, SWAP))
    lengths, mine = lax.optimization_barrier((lengths, mine))
    first_keys, values = turned_values(lengths, cache_keys, cache_values)
    piece = lax.dynamic_index_in_dim(exchange(mine, PLANE), span_owner[0] // 2, 0, False)
    piece, first_keys, values = lax.optimization_barrier((piece, first_keys, values))

    own_away = exchange(jnp.broadcast_to(piece[None], (PIECES, PIECE, HEAD)), TEAMS)
    other_away = lax.ppermute(own_away, AXIS, SWAP)
    own_here = lax.ppermute(own_away, AXIS, PAIR)

    part, keys = first_attention(own_away, first_keys, cache_keys, values)
    attend = functools.partial(attention, keys=keys, values=values)
    part, other_away, own_here = lax.optimization_barrier((part, other_away, own_here))
    peer_away = lax.ppermute(part, AXIS, SWAP)
    other_here = lax.ppermute(own_here, AXIS, SWAP)
    part = attend(other_away)
    away = merge(part, peer_away)
    away, other_here = lax.optimization_barrier((away, other_here))
    here = lax.ppermute(away, AXIS, CROSS)
    part = attend(other_here)
    peer_here = lax.ppermute(part, AXIS, SWAP)
    part, own_here = lax.optimization_barrier((part, own_here))
    part = attend(own_here)

    received = exchange(merge(part, peer_here, merge(here)), TEAMS)
    result = exchange(finish(received), PLANE)
    out = place(span_owner, result, lax.ppermute(result, AXIS, SWAP))
    return out[None]


def solution(mesh):
    return jax.shard_map(
        per_device,
        mesh=mesh,
        in_specs=(P("seq", None, "head"), P("seq", "head"), P("seq", "head"), P(), P()),
        out_specs=P("seq", None, "head"),
        check_vma=False,
    )
```

```python
import functools
import math

import jax
import jax.numpy as jnp
from jax import lax
from jax.experimental import pallas as pl
from jax.experimental.pallas import tpu as pltpu
from jax.sharding import PartitionSpec as P

AXIS = "seq"
CHIPS = 16
HEAD = 128
PIECE = 64
TAIL = 8
ROWS = PIECE + TAIL
VROWS = HEAD + 16
COLUMNS = 4
BLOCK = 512
PIECES = 2 * BLOCK // HEAD
STEP = 512
CHUNK = 2048
BF16 = jnp.bfloat16
F32 = jnp.float32
LOG2_SCALE = math.log2(math.e) / math.sqrt(HEAD)
NT = (((1,), (1,)), ((), ()))

SWAP = [(i, i ^ 1) for i in range(2 * CHIPS)]
PLANE = [[2 * chip + core for chip in range(CHIPS)] for core in range(2)]


def device(y, x, core):
    return (y * COLUMNS + x % COLUMNS) * 2 + core


def partner(y, x, core):
    return device(y, x + (1 if (x + core) % 2 == 0 else -1), core)


EVERY = [(y, x, core) for y in range(COLUMNS) for x in range(COLUMNS) for core in range(2)]
PAIR = [(device(*place), partner(*place)) for place in EVERY]
CROSS = [(device(y, x, 1 - core), partner(y, x, core)) for y, x, core in EVERY]
COLUMNS_OF = (((0, 3), (1, 2)), ((0, 1), (2, 3)))
TEAMS = [
    [device(y, x, core) for y in range(COLUMNS) for x in columns]
    for core in range(2)
    for columns in COLUMNS_OF[core]
]


def member(chip, core):
    y, x = divmod(chip, COLUMNS)
    team = 0 if x in COLUMNS_OF[core][0] else 1
    return team, 2 * y + COLUMNS_OF[core][team].index(x)


def vmem(limit):
    return pltpu.CompilerParams(vmem_limit_bytes=limit << 20)


def exchange(pieces, groups):
    return lax.all_to_all(pieces, AXIS, 0, 0, axis_index_groups=groups, tiled=True)


def in_hbm(array):
    return pltpu.with_memory_space_constraint(array, pltpu.HBM)


def values_kernel(len_ref, k_ref, v_ref, head_ref, o_ref, held_ref, sems):
    spans = [slice(start, start + CHUNK) for start in range(0, v_ref.shape[0], CHUNK)]
    copies = [
        pltpu.make_async_copy(v_ref.at[span], held_ref.at[span], sems.at[i])
        for i, span in enumerate(spans)
    ]
    copies.append(pltpu.make_async_copy(k_ref.at[spans[0]], head_ref, sems.at[len(spans)]))
    for copy in copies:
        copy.start()
    lanes = lax.broadcasted_iota(jnp.int32, (HEAD, HEAD), 1)
    eye = (lanes == lax.broadcasted_iota(jnp.int32, (HEAD, HEAD), 0)).astype(BF16)
    valid_len = len_ref[lax.axis_index(AXIS)]
    for copy, span in zip(copies, spans):
        copy.wait()
        turned = lax.dot_general(eye, held_ref[span, :], NT, preferred_element_type=F32)
        valid = span.start + lax.broadcasted_iota(jnp.int32, (1, CHUNK), 1) < valid_len
        o_ref[:HEAD, span] = jnp.where(valid, turned, 0.0).astype(BF16)
        ones = jnp.broadcast_to(jnp.where(valid, 1.0, 0.0), (VROWS - HEAD, CHUNK))
        o_ref[HEAD:, span] = ones.astype(BF16)
    copies[-1].wait()


def turned_values(lengths, keys, values):
    count = values.shape[0]
    hbm_spec = pl.BlockSpec(memory_space=pltpu.HBM)
    vmem_spec = pl.BlockSpec(memory_space=pltpu.VMEM)
    return pl.pallas_call(
        values_kernel,
        out_shape=(
            jax.ShapeDtypeStruct((CHUNK, HEAD), BF16),
            jax.ShapeDtypeStruct((VROWS, count), BF16),
        ),
        in_specs=[pl.BlockSpec(memory_space=pltpu.SMEM), hbm_spec, hbm_spec],
        out_specs=(vmem_spec, vmem_spec),
        scratch_shapes=[
            pltpu.VMEM(values.shape, BF16),
            pltpu.SemaphoreType.DMA((count // CHUNK + 1,)),
        ],
        compiler_params=vmem(16),
        cost_estimate=pl.CostEstimate(
            flops=4 * count * HEAD * HEAD, bytes_accessed=5 * count * HEAD, transcendentals=0
        ),
        name="turn_values",
    )(lengths, in_hbm(keys), in_hbm(values))


def write_block(o_ref, out, sums, top):
    row = lax.broadcasted_iota(jnp.int32, (TAIL, HEAD), 0)
    for head in range(BLOCK // HEAD):
        lanes = slice(head * HEAD, (head + 1) * HEAD)
        tail = jnp.where(row < TAIL // 2, sums[:, lanes], top[:, lanes])
        for part in range(2):
            o_ref[2 * head + part, :PIECE, :] = out[part * PIECE : (part + 1) * PIECE, lanes]
            o_ref[2 * head + part, PIECE:, :] = tail


def weigh(q, keys, values):
    scores = lax.dot_general(keys, q, NT, preferred_element_type=F32)
    weights = jnp.exp2(scores * LOG2_SCALE).astype(BF16)
    return jnp.dot(values, weights, preferred_element_type=F32)


def settle(total, q, k_ref, v_ref, o_ref, acc_ref):
    sums = total[HEAD : HEAD + 1, :]
    write_block(o_ref, total[:HEAD], sums, jnp.zeros_like(sums))
    good = (sums >= 2.0**-10) & (sums <= 2.0**20)
    bad = jnp.max(jnp.where(jnp.abs(total[:HEAD]) < 3e38, 0.0, 1.0), axis=0, keepdims=True)
    fine = jnp.max(jnp.where(good, bad, 1.0)) < 0.5

    @pl.when(jnp.logical_not(fine))
    def _():
        acc_ref[...] = jnp.zeros_like(acc_ref)
        valid_len = jnp.sum(v_ref[HEAD : HEAD + 1, :].astype(F32)).astype(jnp.int32)

        def body(i, top):
            at = pl.multiple_of(i * STEP, STEP)
            s = lax.dot_general(k_ref[pl.ds(at, STEP), :], q, NT, preferred_element_type=F32)
            row = at + lax.broadcasted_iota(jnp.int32, (STEP, 1), 0)
            s = jnp.where(row < valid_len, s * LOG2_SCALE, -jnp.inf)
            new_top = jnp.maximum(top, jnp.max(s, axis=0, keepdims=True))
            w = jnp.exp2(s - new_top).astype(BF16)
            part = jnp.dot(v_ref[:, pl.ds(at, STEP)], w, preferred_element_type=F32)
            acc_ref[...] = acc_ref[...] * jnp.exp2(top - new_top) + part
            return new_top

        start_top = jnp.full((1, BLOCK), -jnp.inf, F32)
        top = lax.fori_loop(0, k_ref.shape[0] // STEP, body, start_top)
        write_block(o_ref, acc_ref[:HEAD, :], acc_ref[HEAD : HEAD + 1, :], top)


def attention_kernel(q_ref, k_ref, v_ref, o_ref, acc_ref):
    q = q_ref[...]
    settle(weigh(q, k_ref[...], v_ref[...]), q, k_ref, v_ref, o_ref, acc_ref)


def first_attention_kernel(q_ref, head_ref, k_ref, v_ref, o_ref, kept_ref, acc_ref, sems):
    spans = [slice(start, start + CHUNK) for start in range(0, k_ref.shape[0], CHUNK)]
    copies = [
        pltpu.make_async_copy(k_ref.at[span] if i else head_ref, kept_ref.at[span], sems.at[i])
        for i, span in enumerate(spans)
    ]
    for copy in copies[1:] + copies[:1]:
        copy.start()
    q = q_ref[...]
    total = weigh(q, head_ref[...], v_ref[:, spans[0]])
    for copy, span in zip(copies[1:], spans[1:]):
        copy.wait()
        total += weigh(q, kept_ref[span, :], v_ref[:, span])
    copies[0].wait()
    settle(total, q, kept_ref, v_ref, o_ref, acc_ref)


def first_attention(rows, head, keys, values):
    vmem_spec = pl.BlockSpec(memory_space=pltpu.VMEM)
    return pl.pallas_call(
        first_attention_kernel,
        out_shape=(
            jax.ShapeDtypeStruct((PIECES, ROWS, HEAD), F32),
            jax.ShapeDtypeStruct(keys.shape, BF16),
        ),
        in_specs=[vmem_spec, vmem_spec, pl.BlockSpec(memory_space=pltpu.HBM), vmem_spec],
        out_specs=(vmem_spec, vmem_spec),
        scratch_shapes=[
            pltpu.VMEM((VROWS, BLOCK), F32),
            pltpu.SemaphoreType.DMA((keys.shape[0] // CHUNK,)),
        ],
        compiler_params=vmem(44),
        cost_estimate=pl.CostEstimate(
            flops=BLOCK * keys.size // 2, bytes_accessed=keys.size, transcendentals=0
        ),
        name="first_attention",
    )(rows.reshape(BLOCK, HEAD), head, in_hbm(keys), values)


def attention(rows, keys, values):
    vmem_spec = pl.BlockSpec(memory_space=pltpu.VMEM)
    return pl.pallas_call(
        attention_kernel,
        out_shape=jax.ShapeDtypeStruct((PIECES, ROWS, HEAD), F32),
        in_specs=[vmem_spec] * 3,
        out_specs=vmem_spec,
        scratch_shapes=[pltpu.VMEM((VROWS, BLOCK), F32)],
        compiler_params=vmem(44),
        cost_estimate=pl.CostEstimate(
            flops=BLOCK * keys.size // 2, bytes_accessed=keys.size, transcendentals=0
        ),
        name="attention",
    )(rows.reshape(BLOCK, HEAD), keys, values)


def merge_kernel(*refs):
    parts, o_ref = refs[:-1], refs[-1]
    tops = [ref[:, ROWS - 1 :, :] for ref in parts]
    top = functools.reduce(jnp.maximum, tops)
    scales = [jnp.exp2(t - top) for t in tops]
    sums = sum(w * ref[:, PIECE : PIECE + 1, :] for w, ref in zip(scales, parts))
    row = lax.broadcasted_iota(jnp.int32, (1, TAIL, HEAD), 1)
    o_ref[:, :PIECE, :] = sum(w * ref[:, :PIECE, :] for w, ref in zip(scales, parts))
    o_ref[:, PIECE:, :] = jnp.where(row < TAIL // 2, sums, top)


def merge(*parts):
    return pl.pallas_call(
        merge_kernel,
        out_shape=jax.ShapeDtypeStruct(parts[0].shape, F32),
        compiler_params=vmem(16),
        name="merge",
    )(*parts)


def split_kernel(q_ref, keep_ref, send_ref, sems):
    half = q_ref.shape[1] // 2

    def put(ref, core, sem):
        copies = []
        for chip in range(CHIPS):
            team, place = member(chip, core)
            head, part = divmod((1 - team) * PIECES + place, 2)
            column = core * half + head * HEAD
            piece = q_ref.at[part * PIECE : (part + 1) * PIECE, column : column + HEAD]
            copies.append(pltpu.make_async_copy(piece, ref.at[chip], sem.at[chip]))
        return copies

    for core in range(2):

        @pl.when(lax.axis_index(AXIS) % 2 == core)
        def _():
            copies = put(send_ref, 1 - core, sems.at[0]) + put(keep_ref, core, sems.at[1])
            for copy in copies:
                copy.start()
            for copy in copies:
                copy.wait()


def split(block):
    shape = jax.ShapeDtypeStruct((CHIPS, PIECE, HEAD), BF16)
    vmem_spec = pl.BlockSpec(memory_space=pltpu.VMEM)
    return pl.pallas_call(
        split_kernel,
        out_shape=(shape, shape),
        in_specs=[pl.BlockSpec(memory_space=pltpu.HBM)],
        out_specs=(vmem_spec, vmem_spec),
        scratch_shapes=[pltpu.SemaphoreType.DMA((2, CHIPS))],
        compiler_params=vmem(16),
        name="split",
    )(in_hbm(block))


def choose_kernel(owner_ref, a_ref, b_ref, o_ref):
    mine = owner_ref[0] % 2 == lax.axis_index(AXIS) % 2

    @pl.when(mine)
    def _():
        o_ref[...] = a_ref[...]

    @pl.when(jnp.logical_not(mine))
    def _():
        o_ref[...] = b_ref[...]


def choose(owner, a, b):
    return pl.pallas_call(
        choose_kernel,
        out_shape=jax.ShapeDtypeStruct(a.shape, a.dtype),
        in_specs=[
            pl.BlockSpec(memory_space=pltpu.SMEM),
            pl.BlockSpec(memory_space=pltpu.VMEM),
            pl.BlockSpec(memory_space=pltpu.VMEM),
        ],
        compiler_params=vmem(16),
        name="choose",
    )(owner, a, b)


def finish_kernel(r_ref, o_ref):
    tops = r_ref[:, ROWS - 1 :, :]
    scale = jnp.exp2(tops - jnp.max(tops, axis=0, keepdims=True))
    denom = jnp.sum(scale * r_ref[:, PIECE : PIECE + 1, :], axis=0)
    numer = jnp.sum(scale * r_ref[:, :PIECE, :], axis=0)
    result = (numer / denom).astype(BF16)
    o_ref[...] = jnp.broadcast_to(result[None], o_ref.shape)


def finish(received):
    return pl.pallas_call(
        finish_kernel,
        out_shape=jax.ShapeDtypeStruct((CHIPS, PIECE, HEAD), BF16),
        compiler_params=vmem(16),
        name="finish",
    )(received)


def place_kernel(owner_ref, a_ref, b_ref, o_ref):
    half = o_ref.shape[1] // 2

    me = lax.axis_index(AXIS)
    wanted = me == owner_ref[0]

    @pl.when(jnp.logical_not(wanted))
    def _():
        o_ref[...] = jnp.zeros_like(o_ref)

    def put(*halves):
        for core, ref in enumerate(halves):
            for team in range(2):
                left, right = COLUMNS_OF[core][team]
                for y in range(COLUMNS):
                    pieces = [ref[y * COLUMNS + x] for x in (left, right)]
                    column = core * half + (team * COLUMNS + y) * HEAD
                    o_ref[:, column : column + HEAD] = jnp.concatenate(pieces, axis=0).T

    @pl.when(wanted & (me % 2 == 0))
    def _():
        put(a_ref, b_ref)

    @pl.when(wanted & (me % 2 == 1))
    def _():
        put(b_ref, a_ref)


def place(owner, own, other):
    return pl.pallas_call(
        place_kernel,
        out_shape=jax.ShapeDtypeStruct((HEAD, 2 * CHIPS * PIECE), BF16),
        in_specs=[
            pl.BlockSpec(memory_space=pltpu.SMEM),
            pl.BlockSpec(memory_space=pltpu.VMEM),
            pl.BlockSpec(memory_space=pltpu.VMEM),
        ],
        compiler_params=vmem(16),
        name="place",
    )(owner, own, other)


def per_device(queries, cache_keys, cache_values, lengths, span_owner):
    keep, send = split(queries[0])
    mine = choose(span_owner, keep, lax.ppermute(send, AXIS, SWAP))
    lengths, mine = lax.optimization_barrier((lengths, mine))
    first_keys, values = turned_values(lengths, cache_keys, cache_values)
    piece = lax.dynamic_index_in_dim(exchange(mine, PLANE), span_owner[0] // 2, 0, False)
    piece, first_keys, values = lax.optimization_barrier((piece, first_keys, values))

    own_away = exchange(jnp.broadcast_to(piece[None], (PIECES, PIECE, HEAD)), TEAMS)
    other_away = lax.ppermute(own_away, AXIS, SWAP)
    own_here = lax.ppermute(own_away, AXIS, PAIR)

    part, keys = first_attention(own_away, first_keys, cache_keys, values)
    attend = functools.partial(attention, keys=keys, values=values)
    part, other_away, own_here = lax.optimization_barrier((part, other_away, own_here))
    peer_away = lax.ppermute(part, AXIS, SWAP)
    other_here = lax.ppermute(own_here, AXIS, SWAP)
    part = attend(other_away)
    away = merge(part, peer_away)
    away, other_here = lax.optimization_barrier((away, other_here))
    here = lax.ppermute(away, AXIS, CROSS)
    part = attend(other_here)
    peer_here = lax.ppermute(part, AXIS, SWAP)
    part, own_here = lax.optimization_barrier((part, own_here))
    part = attend(own_here)

    received = exchange(merge(part, peer_here, merge(here)), TEAMS)
    result = exchange(finish(received), PLANE)
    out = place(span_owner, result, lax.ppermute(result, AXIS, SWAP))
    return out[None]


def solution(mesh):
    return jax.shard_map(
        per_device,
        mesh=mesh,
        in_specs=(P("seq", None, "head"), P("seq", "head"), P("seq", "head"), P(), P()),
        out_specs=P("seq", None, "head"),
        check_vma=False,
    )
```

```python
import functools
import math

import jax
import jax.numpy as jnp
from jax import lax
from jax.experimental import pallas as pl
from jax.experimental.pallas import tpu as pltpu
from jax.sharding import PartitionSpec as P

AXIS = "seq"
CHIPS = 16
HEAD = 128
PIECE = 64
TAIL = 8
ROWS = PIECE + TAIL
VROWS = HEAD + 16
COLUMNS = 4
BLOCK = 512
PIECES = 2 * BLOCK // HEAD
STEP = 512
CHUNK = 2048
BF16 = jnp.bfloat16
F32 = jnp.float32
LOG2_SCALE = math.log2(math.e) / math.sqrt(HEAD)
NT = (((1,), (1,)), ((), ()))

SWAP = [(i, i ^ 1) for i in range(2 * CHIPS)]


def snake(chip):
    y, x = divmod(chip, COLUMNS)
    return y * COLUMNS + (COLUMNS - 1 - x if y % 2 else x)


PLANE = [[2 * snake(place) + core for place in range(CHIPS)] for core in range(2)]


def device(y, x, core):
    return (y % COLUMNS * COLUMNS + x % COLUMNS) * 2 + core


def partner(y, x, core):
    if core == 0:
        return device(y + (1 if y % 2 else -1), x, core)
    return device(y, x + (1 if x % 2 else -1), core)


EVERY = [(y, x, core) for y in range(COLUMNS) for x in range(COLUMNS) for core in range(2)]
PAIR = [(device(*place), partner(*place)) for place in EVERY]
CROSS = [(device(y, x, 1 - core), partner(y, x, core)) for y, x, core in EVERY]
def member(chip, core):
    y, x = divmod(chip, COLUMNS)
    short, long = (y, x) if core == 0 else (x, y)
    return short // 2, 2 * long + short % 2


SEATS = [
    [sorted((c for c in range(CHIPS) if member(c, core)[0] == team), key=lambda c: member(c, core)[1])
     for team in range(2)]
    for core in range(2)
]
TEAMS = [[2 * chip + core for chip in SEATS[core][team]] for core in range(2) for team in range(2)]


def vmem(limit):
    return pltpu.CompilerParams(vmem_limit_bytes=limit << 20)


def exchange(pieces, groups):
    return lax.all_to_all(pieces, AXIS, 0, 0, axis_index_groups=groups, tiled=True)


def in_hbm(array):
    return pltpu.with_memory_space_constraint(array, pltpu.HBM)


def values_kernel(len_ref, k_ref, v_ref, head_ref, o_ref, held_ref, sems):
    spans = [slice(start, start + CHUNK) for start in range(0, v_ref.shape[0], CHUNK)]
    copies = [
        pltpu.make_async_copy(v_ref.at[span], held_ref.at[span], sems.at[i])
        for i, span in enumerate(spans)
    ]
    copies.append(pltpu.make_async_copy(k_ref.at[spans[0]], head_ref, sems.at[len(spans)]))
    for copy in copies:
        copy.start()
    lanes = lax.broadcasted_iota(jnp.int32, (HEAD, HEAD), 1)
    eye = (lanes == lax.broadcasted_iota(jnp.int32, (HEAD, HEAD), 0)).astype(BF16)
    valid_len = len_ref[lax.axis_index(AXIS)]
    for copy, span in zip(copies, spans):
        copy.wait()
        turned = lax.dot_general(eye, held_ref[span, :], NT, preferred_element_type=F32)
        valid = span.start + lax.broadcasted_iota(jnp.int32, (1, CHUNK), 1) < valid_len
        o_ref[:HEAD, span] = jnp.where(valid, turned, 0.0).astype(BF16)
        ones = jnp.broadcast_to(jnp.where(valid, 1.0, 0.0), (VROWS - HEAD, CHUNK))
        o_ref[HEAD:, span] = ones.astype(BF16)
    copies[-1].wait()


def turned_values(lengths, keys, values):
    count = values.shape[0]
    hbm_spec = pl.BlockSpec(memory_space=pltpu.HBM)
    vmem_spec = pl.BlockSpec(memory_space=pltpu.VMEM)
    return pl.pallas_call(
        values_kernel,
        out_shape=(
            jax.ShapeDtypeStruct((CHUNK, HEAD), BF16),
            jax.ShapeDtypeStruct((VROWS, count), BF16),
        ),
        in_specs=[pl.BlockSpec(memory_space=pltpu.SMEM), hbm_spec, hbm_spec],
        out_specs=(vmem_spec, vmem_spec),
        scratch_shapes=[
            pltpu.VMEM(values.shape, BF16),
            pltpu.SemaphoreType.DMA((count // CHUNK + 1,)),
        ],
        compiler_params=vmem(16),
        cost_estimate=pl.CostEstimate(
            flops=4 * count * HEAD * HEAD, bytes_accessed=5 * count * HEAD, transcendentals=0
        ),
        name="turn_values",
    )(lengths, in_hbm(keys), in_hbm(values))


def write_block(o_ref, out, sums, top):
    row = lax.broadcasted_iota(jnp.int32, (TAIL, HEAD), 0)
    for head in range(BLOCK // HEAD):
        lanes = slice(head * HEAD, (head + 1) * HEAD)
        tail = jnp.where(row < TAIL // 2, sums[:, lanes], top[:, lanes])
        for part in range(2):
            o_ref[2 * head + part, :PIECE, :] = out[part * PIECE : (part + 1) * PIECE, lanes]
            o_ref[2 * head + part, PIECE:, :] = tail


def weigh(q, keys, values):
    scores = lax.dot_general(keys, q, NT, preferred_element_type=F32)
    weights = jnp.exp2(scores * LOG2_SCALE).astype(BF16)
    return jnp.dot(values, weights, preferred_element_type=F32)


def settle(total, q, k_ref, v_ref, o_ref, acc_ref):
    sums = total[HEAD : HEAD + 1, :]
    write_block(o_ref, total[:HEAD], sums, jnp.zeros_like(sums))
    good = (sums >= 2.0**-10) & (sums <= 2.0**20)
    bad = jnp.max(jnp.where(jnp.abs(total[:HEAD]) < 3e38, 0.0, 1.0), axis=0, keepdims=True)
    fine = jnp.max(jnp.where(good, bad, 1.0)) < 0.5

    @pl.when(jnp.logical_not(fine))
    def _():
        acc_ref[...] = jnp.zeros_like(acc_ref)
        valid_len = jnp.sum(v_ref[HEAD : HEAD + 1, :].astype(F32)).astype(jnp.int32)

        def body(i, top):
            at = pl.multiple_of(i * STEP, STEP)
            s = lax.dot_general(k_ref[pl.ds(at, STEP), :], q, NT, preferred_element_type=F32)
            row = at + lax.broadcasted_iota(jnp.int32, (STEP, 1), 0)
            s = jnp.where(row < valid_len, s * LOG2_SCALE, -jnp.inf)
            new_top = jnp.maximum(top, jnp.max(s, axis=0, keepdims=True))
            w = jnp.exp2(s - new_top).astype(BF16)
            part = jnp.dot(v_ref[:, pl.ds(at, STEP)], w, preferred_element_type=F32)
            acc_ref[...] = acc_ref[...] * jnp.exp2(top - new_top) + part
            return new_top

        start_top = jnp.full((1, BLOCK), -jnp.inf, F32)
        top = lax.fori_loop(0, k_ref.shape[0] // STEP, body, start_top)
        write_block(o_ref, acc_ref[:HEAD, :], acc_ref[HEAD : HEAD + 1, :], top)


def attention_kernel(q_ref, k_ref, v_ref, o_ref, acc_ref):
    q = q_ref[...]
    settle(weigh(q, k_ref[...], v_ref[...]), q, k_ref, v_ref, o_ref, acc_ref)


def first_attention_kernel(q_ref, head_ref, k_ref, v_ref, o_ref, kept_ref, acc_ref, sems):
    spans = [slice(start, start + CHUNK) for start in range(0, k_ref.shape[0], CHUNK)]
    copies = [
        pltpu.make_async_copy(k_ref.at[span] if i else head_ref, kept_ref.at[span], sems.at[i])
        for i, span in enumerate(spans)
    ]
    for copy in copies[1:] + copies[:1]:
        copy.start()
    q = q_ref[...]
    total = weigh(q, head_ref[...], v_ref[:, spans[0]])
    for copy, span in zip(copies[1:], spans[1:]):
        copy.wait()
        total += weigh(q, kept_ref[span, :], v_ref[:, span])
    copies[0].wait()
    settle(total, q, kept_ref, v_ref, o_ref, acc_ref)


def first_attention(rows, head, keys, values):
    vmem_spec = pl.BlockSpec(memory_space=pltpu.VMEM)
    return pl.pallas_call(
        first_attention_kernel,
        out_shape=(
            jax.ShapeDtypeStruct((PIECES, ROWS, HEAD), F32),
            jax.ShapeDtypeStruct(keys.shape, BF16),
        ),
        in_specs=[vmem_spec, vmem_spec, pl.BlockSpec(memory_space=pltpu.HBM), vmem_spec],
        out_specs=(vmem_spec, vmem_spec),
        scratch_shapes=[
            pltpu.VMEM((VROWS, BLOCK), F32),
            pltpu.SemaphoreType.DMA((keys.shape[0] // CHUNK,)),
        ],
        compiler_params=vmem(44),
        cost_estimate=pl.CostEstimate(
            flops=BLOCK * keys.size // 2, bytes_accessed=keys.size, transcendentals=0
        ),
        name="first_attention",
    )(rows.reshape(BLOCK, HEAD), head, in_hbm(keys), values)


def attention(rows, keys, values):
    vmem_spec = pl.BlockSpec(memory_space=pltpu.VMEM)
    return pl.pallas_call(
        attention_kernel,
        out_shape=jax.ShapeDtypeStruct((PIECES, ROWS, HEAD), F32),
        in_specs=[vmem_spec] * 3,
        out_specs=vmem_spec,
        scratch_shapes=[pltpu.VMEM((VROWS, BLOCK), F32)],
        compiler_params=vmem(44),
        cost_estimate=pl.CostEstimate(
            flops=BLOCK * keys.size // 2, bytes_accessed=keys.size, transcendentals=0
        ),
        name="attention",
    )(rows.reshape(BLOCK, HEAD), keys, values)


def merge_kernel(*refs):
    parts, o_ref = refs[:-1], refs[-1]
    tops = [ref[:, ROWS - 1 :, :] for ref in parts]
    top = functools.reduce(jnp.maximum, tops)
    scales = [jnp.exp2(t - top) for t in tops]
    sums = sum(w * ref[:, PIECE : PIECE + 1, :] for w, ref in zip(scales, parts))
    row = lax.broadcasted_iota(jnp.int32, (1, TAIL, HEAD), 1)
    o_ref[:, :PIECE, :] = sum(w * ref[:, :PIECE, :] for w, ref in zip(scales, parts))
    o_ref[:, PIECE:, :] = jnp.where(row < TAIL // 2, sums, top)


def merge(*parts):
    return pl.pallas_call(
        merge_kernel,
        out_shape=jax.ShapeDtypeStruct(parts[0].shape, F32),
        compiler_params=vmem(16),
        name="merge",
    )(*parts)


def split_kernel(q_ref, keep_ref, send_ref, sems):
    half = q_ref.shape[1] // 2

    def put(ref, core, sem):
        copies = []
        for chip in range(CHIPS):
            team, place = member(chip, core)
            head, part = divmod((1 - team) * PIECES + place, 2)
            column = core * half + head * HEAD
            piece = q_ref.at[part * PIECE : (part + 1) * PIECE, column : column + HEAD]
            copies.append(pltpu.make_async_copy(piece, ref.at[snake(chip)], sem.at[chip]))
        return copies

    for core in range(2):

        @pl.when(lax.axis_index(AXIS) % 2 == core)
        def _():
            copies = put(send_ref, 1 - core, sems.at[0]) + put(keep_ref, core, sems.at[1])
            for copy in copies:
                copy.start()
            for copy in copies:
                copy.wait()


def split(block):
    shape = jax.ShapeDtypeStruct((CHIPS, PIECE, HEAD), BF16)
    vmem_spec = pl.BlockSpec(memory_space=pltpu.VMEM)
    return pl.pallas_call(
        split_kernel,
        out_shape=(shape, shape),
        in_specs=[pl.BlockSpec(memory_space=pltpu.HBM)],
        out_specs=(vmem_spec, vmem_spec),
        scratch_shapes=[pltpu.SemaphoreType.DMA((2, CHIPS))],
        compiler_params=vmem(16),
        name="split",
    )(in_hbm(block))


def choose_kernel(owner_ref, a_ref, b_ref, o_ref):
    mine = owner_ref[0] % 2 == lax.axis_index(AXIS) % 2

    @pl.when(mine)
    def _():
        o_ref[...] = a_ref[...]

    @pl.when(jnp.logical_not(mine))
    def _():
        o_ref[...] = b_ref[...]


def choose(owner, a, b):
    return pl.pallas_call(
        choose_kernel,
        out_shape=jax.ShapeDtypeStruct(a.shape, a.dtype),
        in_specs=[
            pl.BlockSpec(memory_space=pltpu.SMEM),
            pl.BlockSpec(memory_space=pltpu.VMEM),
            pl.BlockSpec(memory_space=pltpu.VMEM),
        ],
        compiler_params=vmem(16),
        name="choose",
    )(owner, a, b)


def finish_kernel(r_ref, o_ref):
    tops = r_ref[:, ROWS - 1 :, :]
    scale = jnp.exp2(tops - jnp.max(tops, axis=0, keepdims=True))
    denom = jnp.sum(scale * r_ref[:, PIECE : PIECE + 1, :], axis=0)
    numer = jnp.sum(scale * r_ref[:, :PIECE, :], axis=0)
    result = (numer / denom).astype(BF16)
    o_ref[...] = jnp.broadcast_to(result[None], o_ref.shape)


def finish(received):
    return pl.pallas_call(
        finish_kernel,
        out_shape=jax.ShapeDtypeStruct((CHIPS, PIECE, HEAD), BF16),
        compiler_params=vmem(16),
        name="finish",
    )(received)


def place_kernel(owner_ref, a_ref, b_ref, o_ref):
    half = o_ref.shape[1] // 2

    me = lax.axis_index(AXIS)
    wanted = me == owner_ref[0]

    @pl.when(jnp.logical_not(wanted))
    def _():
        o_ref[...] = jnp.zeros_like(o_ref)

    def put(*halves):
        for core, ref in enumerate(halves):
            for team in range(2):
                chips = SEATS[core][team]
                for spot in range(0, PIECES, 2):
                    pieces = [ref[snake(chip)] for chip in chips[spot : spot + 2]]
                    column = core * half + (team * PIECES + spot) // 2 * HEAD
                    o_ref[:, column : column + HEAD] = jnp.concatenate(pieces, axis=0).T

    @pl.when(wanted & (me % 2 == 0))
    def _():
        put(a_ref, b_ref)

    @pl.when(wanted & (me % 2 == 1))
    def _():
        put(b_ref, a_ref)


def place(owner, own, other):
    return pl.pallas_call(
        place_kernel,
        out_shape=jax.ShapeDtypeStruct((HEAD, 2 * CHIPS * PIECE), BF16),
        in_specs=[
            pl.BlockSpec(memory_space=pltpu.SMEM),
            pl.BlockSpec(memory_space=pltpu.VMEM),
            pl.BlockSpec(memory_space=pltpu.VMEM),
        ],
        compiler_params=vmem(16),
        name="place",
    )(owner, own, other)


def per_device(queries, cache_keys, cache_values, lengths, span_owner):
    keep, send = split(queries[0])
    mine = choose(span_owner, keep, lax.ppermute(send, AXIS, SWAP))
    lengths, mine = lax.optimization_barrier((lengths, mine))
    first_keys, values = turned_values(lengths, cache_keys, cache_values)
    y, x = span_owner[0] // (2 * COLUMNS), span_owner[0] // 2 % COLUMNS
    slot = y * COLUMNS + jnp.where(y % 2 == 1, COLUMNS - 1 - x, x)
    piece = lax.dynamic_index_in_dim(exchange(mine, PLANE), slot, 0, False)
    piece, first_keys, values = lax.optimization_barrier((piece, first_keys, values))

    own_away = exchange(jnp.broadcast_to(piece[None], (PIECES, PIECE, HEAD)), TEAMS)
    other_away = lax.ppermute(own_away, AXIS, SWAP)
    own_here = lax.ppermute(own_away, AXIS, PAIR)

    part, keys = first_attention(own_away, first_keys, cache_keys, values)
    attend = functools.partial(attention, keys=keys, values=values)
    part, other_away, own_here = lax.optimization_barrier((part, other_away, own_here))
    peer_away = lax.ppermute(part, AXIS, SWAP)
    other_here = lax.ppermute(own_here, AXIS, SWAP)
    part = attend(other_away)
    away = merge(part, peer_away)
    away, other_here = lax.optimization_barrier((away, other_here))
    here = lax.ppermute(away, AXIS, CROSS)
    part = attend(other_here)
    peer_here = lax.ppermute(part, AXIS, SWAP)
    part, own_here = lax.optimization_barrier((part, own_here))
    part = attend(own_here)

    received = exchange(merge(part, peer_here, merge(here)), TEAMS)
    result = exchange(finish(received), PLANE)
    out = place(span_owner, result, lax.ppermute(result, AXIS, SWAP))
    return out[None]


def solution(mesh):
    return jax.shard_map(
        per_device,
        mesh=mesh,
        in_specs=(P("seq", None, "head"), P("seq", "head"), P("seq", "head"), P(), P()),
        out_specs=P("seq", None, "head"),
        check_vma=False,
    )
```

```python
import functools
import math

import jax
import jax.numpy as jnp
from jax import lax
from jax.experimental import pallas as pl
from jax.experimental.pallas import tpu as pltpu
from jax.sharding import PartitionSpec as P

AXIS = "seq"
CHIPS = 16
HEAD = 128
PIECE = 64
TAIL = 8
ROWS = PIECE + TAIL
VROWS = HEAD + 16
COLUMNS = 4
BLOCK = 512
PIECES = 2 * BLOCK // HEAD
STEP = 512
CHUNK = 2048
BF16 = jnp.bfloat16
F32 = jnp.float32
LOG2_SCALE = math.log2(math.e) / math.sqrt(HEAD)
NT = (((1,), (1,)), ((), ()))

SWAP = [(i, i ^ 1) for i in range(2 * CHIPS)]


def snake(chip):
    y, x = divmod(chip, COLUMNS)
    return y * COLUMNS + (COLUMNS - 1 - x if y % 2 else x)


PLANE = [[2 * snake(place) + core for place in range(CHIPS)] for core in range(2)]


def device(y, x, core):
    return (y % COLUMNS * COLUMNS + x % COLUMNS) * 2 + core


def partner(y, x, core):
    if core == 0:
        return device(y + (1 if y % 2 else -1), x, core)
    return device(y, x + (1 if x % 2 else -1), core)


EVERY = [(y, x, core) for y in range(COLUMNS) for x in range(COLUMNS) for core in range(2)]
PAIR = [(device(*place), partner(*place)) for place in EVERY]
CROSS = [(device(y, x, 1 - core), partner(y, x, core)) for y, x, core in EVERY]
def member(chip, core):
    y, x = divmod(chip, COLUMNS)
    short, long = (y, x) if core == 0 else (x, y)
    return short // 2, 2 * long + short % 2


SEATS = [
    [sorted((c for c in range(CHIPS) if member(c, core)[0] == team), key=lambda c: member(c, core)[1])
     for team in range(2)]
    for core in range(2)
]
TEAMS = [[2 * chip + core for chip in SEATS[core][team]] for core in range(2) for team in range(2)]


def vmem(limit):
    return pltpu.CompilerParams(vmem_limit_bytes=limit << 20)


def exchange(pieces, groups):
    return lax.all_to_all(pieces, AXIS, 0, 0, axis_index_groups=groups, tiled=True)


def in_hbm(array):
    return pltpu.with_memory_space_constraint(array, pltpu.HBM)


def values_kernel(len_ref, k_ref, v_ref, head_ref, o_ref, blank_ref, held_ref, zero_ref, sems):
    spans = [slice(start, start + CHUNK) for start in range(0, v_ref.shape[0], CHUNK)]
    copies = [
        pltpu.make_async_copy(v_ref.at[span], held_ref.at[span], sems.at[i])
        for i, span in enumerate(spans)
    ]
    copies.append(pltpu.make_async_copy(k_ref.at[spans[0]], head_ref, sems.at[len(spans)]))
    for copy in copies:
        copy.start()
    zero_ref[...] = jnp.zeros_like(zero_ref)
    blank = pltpu.make_async_copy(zero_ref, blank_ref, sems.at[len(spans) + 1])
    blank.start()
    lanes = lax.broadcasted_iota(jnp.int32, (HEAD, HEAD), 1)
    eye = (lanes == lax.broadcasted_iota(jnp.int32, (HEAD, HEAD), 0)).astype(BF16)
    valid_len = len_ref[lax.axis_index(AXIS)]
    for copy, span in zip(copies, spans):
        copy.wait()
        turned = lax.dot_general(eye, held_ref[span, :], NT, preferred_element_type=F32)
        valid = span.start + lax.broadcasted_iota(jnp.int32, (1, CHUNK), 1) < valid_len
        o_ref[:HEAD, span] = jnp.where(valid, turned, 0.0).astype(BF16)
        ones = jnp.broadcast_to(jnp.where(valid, 1.0, 0.0), (VROWS - HEAD, CHUNK))
        o_ref[HEAD:, span] = ones.astype(BF16)
    copies[-1].wait()
    blank.wait()


def turned_values(lengths, keys, values, shape):
    count = values.shape[0]
    hbm_spec = pl.BlockSpec(memory_space=pltpu.HBM)
    vmem_spec = pl.BlockSpec(memory_space=pltpu.VMEM)
    return pl.pallas_call(
        values_kernel,
        out_shape=(
            jax.ShapeDtypeStruct((CHUNK, HEAD), BF16),
            jax.ShapeDtypeStruct((VROWS, count), BF16),
            jax.ShapeDtypeStruct(shape, BF16),
        ),
        in_specs=[pl.BlockSpec(memory_space=pltpu.SMEM), hbm_spec, hbm_spec],
        out_specs=(vmem_spec, vmem_spec, hbm_spec),
        scratch_shapes=[
            pltpu.VMEM(values.shape, BF16),
            pltpu.VMEM(shape, BF16),
            pltpu.SemaphoreType.DMA((count // CHUNK + 2,)),
        ],
        compiler_params=vmem(16),
        cost_estimate=pl.CostEstimate(
            flops=4 * count * HEAD * HEAD, bytes_accessed=5 * count * HEAD, transcendentals=0
        ),
        name="turn_values",
    )(lengths, in_hbm(keys), in_hbm(values))


def write_block(o_ref, out, sums, top):
    row = lax.broadcasted_iota(jnp.int32, (TAIL, HEAD), 0)
    for head in range(BLOCK // HEAD):
        lanes = slice(head * HEAD, (head + 1) * HEAD)
        tail = jnp.where(row < TAIL // 2, sums[:, lanes], top[:, lanes])
        for part in range(2):
            o_ref[2 * head + part, :PIECE, :] = out[part * PIECE : (part + 1) * PIECE, lanes]
            o_ref[2 * head + part, PIECE:, :] = tail


def weigh(q, keys, values):
    scores = lax.dot_general(keys, q, NT, preferred_element_type=F32)
    weights = jnp.exp2(scores * LOG2_SCALE).astype(BF16)
    return jnp.dot(values, weights, preferred_element_type=F32)


def settle(total, q, k_ref, v_ref, o_ref, acc_ref):
    sums = total[HEAD : HEAD + 1, :]
    write_block(o_ref, total[:HEAD], sums, jnp.zeros_like(sums))
    good = (sums >= 2.0**-10) & (sums <= 2.0**20)
    bad = jnp.max(jnp.where(jnp.abs(total[:HEAD]) < 3e38, 0.0, 1.0), axis=0, keepdims=True)
    fine = jnp.max(jnp.where(good, bad, 1.0)) < 0.5

    @pl.when(jnp.logical_not(fine))
    def _():
        acc_ref[...] = jnp.zeros_like(acc_ref)
        valid_len = jnp.sum(v_ref[HEAD : HEAD + 1, :].astype(F32)).astype(jnp.int32)

        def body(i, top):
            at = pl.multiple_of(i * STEP, STEP)
            s = lax.dot_general(k_ref[pl.ds(at, STEP), :], q, NT, preferred_element_type=F32)
            row = at + lax.broadcasted_iota(jnp.int32, (STEP, 1), 0)
            s = jnp.where(row < valid_len, s * LOG2_SCALE, -jnp.inf)
            new_top = jnp.maximum(top, jnp.max(s, axis=0, keepdims=True))
            w = jnp.exp2(s - new_top).astype(BF16)
            part = jnp.dot(v_ref[:, pl.ds(at, STEP)], w, preferred_element_type=F32)
            acc_ref[...] = acc_ref[...] * jnp.exp2(top - new_top) + part
            return new_top

        start_top = jnp.full((1, BLOCK), -jnp.inf, F32)
        top = lax.fori_loop(0, k_ref.shape[0] // STEP, body, start_top)
        write_block(o_ref, acc_ref[:HEAD, :], acc_ref[HEAD : HEAD + 1, :], top)


def attention_kernel(q_ref, k_ref, v_ref, o_ref, acc_ref):
    q = q_ref[...]
    settle(weigh(q, k_ref[...], v_ref[...]), q, k_ref, v_ref, o_ref, acc_ref)


def first_attention_kernel(q_ref, head_ref, k_ref, v_ref, o_ref, kept_ref, acc_ref, sems):
    stops = [0, CHUNK, 2 * CHUNK, k_ref.shape[0]]
    spans = [slice(*ends) for ends in zip(stops, stops[1:])]
    copies = [
        pltpu.make_async_copy(k_ref.at[span] if i else head_ref, kept_ref.at[span], sems.at[i])
        for i, span in enumerate(spans)
    ]
    for copy in copies[1:] + copies[:1]:
        copy.start()
    q = q_ref[...]
    total = weigh(q, head_ref[...], v_ref[:, spans[0]])
    for copy, span in zip(copies[1:], spans[1:]):
        copy.wait()
        total += weigh(q, kept_ref[span, :], v_ref[:, span])
    copies[0].wait()
    settle(total, q, kept_ref, v_ref, o_ref, acc_ref)


def first_attention(rows, head, keys, values):
    vmem_spec = pl.BlockSpec(memory_space=pltpu.VMEM)
    return pl.pallas_call(
        first_attention_kernel,
        out_shape=(
            jax.ShapeDtypeStruct((PIECES, ROWS, HEAD), F32),
            jax.ShapeDtypeStruct(keys.shape, BF16),
        ),
        in_specs=[vmem_spec, vmem_spec, pl.BlockSpec(memory_space=pltpu.HBM), vmem_spec],
        out_specs=(vmem_spec, vmem_spec),
        scratch_shapes=[
            pltpu.VMEM((VROWS, BLOCK), F32),
            pltpu.SemaphoreType.DMA((3,)),
        ],
        compiler_params=vmem(44),
        cost_estimate=pl.CostEstimate(
            flops=BLOCK * keys.size // 2, bytes_accessed=keys.size, transcendentals=0
        ),
        name="first_attention",
    )(rows.reshape(BLOCK, HEAD), head, in_hbm(keys), values)


def attention(rows, keys, values):
    vmem_spec = pl.BlockSpec(memory_space=pltpu.VMEM)
    return pl.pallas_call(
        attention_kernel,
        out_shape=jax.ShapeDtypeStruct((PIECES, ROWS, HEAD), F32),
        in_specs=[vmem_spec] * 3,
        out_specs=vmem_spec,
        scratch_shapes=[pltpu.VMEM((VROWS, BLOCK), F32)],
        compiler_params=vmem(44),
        cost_estimate=pl.CostEstimate(
            flops=BLOCK * keys.size // 2, bytes_accessed=keys.size, transcendentals=0
        ),
        name="attention",
    )(rows.reshape(BLOCK, HEAD), keys, values)


def merge_kernel(*refs):
    parts, o_ref = refs[:-1], refs[-1]
    tops = [ref[:, ROWS - 1 :, :] for ref in parts]
    top = functools.reduce(jnp.maximum, tops)
    scales = [jnp.exp2(t - top) for t in tops]
    sums = sum(w * ref[:, PIECE : PIECE + 1, :] for w, ref in zip(scales, parts))
    row = lax.broadcasted_iota(jnp.int32, (1, TAIL, HEAD), 1)
    o_ref[:, :PIECE, :] = sum(w * ref[:, :PIECE, :] for w, ref in zip(scales, parts))
    o_ref[:, PIECE:, :] = jnp.where(row < TAIL // 2, sums, top)


def merge(*parts):
    return pl.pallas_call(
        merge_kernel,
        out_shape=jax.ShapeDtypeStruct(parts[0].shape, F32),
        compiler_params=vmem(16),
        name="merge",
    )(*parts)


def split_kernel(q_ref, keep_ref, send_ref, sems):
    half = q_ref.shape[1] // 2

    def put(ref, core, sem):
        copies = []
        for chip in range(CHIPS):
            team, place = member(chip, core)
            head, part = divmod((1 - team) * PIECES + place, 2)
            column = core * half + head * HEAD
            piece = q_ref.at[part * PIECE : (part + 1) * PIECE, column : column + HEAD]
            copies.append(pltpu.make_async_copy(piece, ref.at[snake(chip)], sem.at[chip]))
        return copies

    for core in range(2):

        @pl.when(lax.axis_index(AXIS) % 2 == core)
        def _():
            copies = put(send_ref, 1 - core, sems.at[0]) + put(keep_ref, core, sems.at[1])
            for copy in copies:
                copy.start()
            for copy in copies:
                copy.wait()


def split(block):
    shape = jax.ShapeDtypeStruct((CHIPS, PIECE, HEAD), BF16)
    vmem_spec = pl.BlockSpec(memory_space=pltpu.VMEM)
    return pl.pallas_call(
        split_kernel,
        out_shape=(shape, shape),
        in_specs=[pl.BlockSpec(memory_space=pltpu.HBM)],
        out_specs=(vmem_spec, vmem_spec),
        scratch_shapes=[pltpu.SemaphoreType.DMA((2, CHIPS))],
        compiler_params=vmem(16),
        name="split",
    )(in_hbm(block))


def choose_kernel(owner_ref, a_ref, b_ref, o_ref):
    mine = owner_ref[0] % 2 == lax.axis_index(AXIS) % 2

    @pl.when(mine)
    def _():
        o_ref[...] = a_ref[...]

    @pl.when(jnp.logical_not(mine))
    def _():
        o_ref[...] = b_ref[...]


def choose(owner, a, b):
    return pl.pallas_call(
        choose_kernel,
        out_shape=jax.ShapeDtypeStruct(a.shape, a.dtype),
        in_specs=[
            pl.BlockSpec(memory_space=pltpu.SMEM),
            pl.BlockSpec(memory_space=pltpu.VMEM),
            pl.BlockSpec(memory_space=pltpu.VMEM),
        ],
        compiler_params=vmem(16),
        name="choose",
    )(owner, a, b)


def finish_kernel(r_ref, o_ref):
    tops = r_ref[:, ROWS - 1 :, :]
    scale = jnp.exp2(tops - jnp.max(tops, axis=0, keepdims=True))
    denom = jnp.sum(scale * r_ref[:, PIECE : PIECE + 1, :], axis=0)
    numer = jnp.sum(scale * r_ref[:, :PIECE, :], axis=0)
    result = (numer / denom).astype(BF16)
    o_ref[...] = jnp.broadcast_to(result[None], o_ref.shape)


def finish(received):
    return pl.pallas_call(
        finish_kernel,
        out_shape=jax.ShapeDtypeStruct((CHIPS, PIECE, HEAD), BF16),
        compiler_params=vmem(16),
        name="finish",
    )(received)


def place_kernel(owner_ref, own_ref, peer_ref, blank_ref, o_ref, held_ref, sem):
    half = held_ref.shape[1] // 2
    me = lax.axis_index(AXIS)

    def put(*halves):
        for core, ref in enumerate(halves):
            for team in range(2):
                chips = SEATS[core][team]
                for spot in range(0, PIECES, 2):
                    pieces = [ref[snake(chip)] for chip in chips[spot : spot + 2]]
                    column = core * half + (team * PIECES + spot) // 2 * HEAD
                    held_ref[:, column : column + HEAD] = jnp.concatenate(pieces, axis=0).T
        copy = pltpu.make_async_copy(held_ref, o_ref, sem)
        copy.start()
        copy.wait()

    @pl.when((me == owner_ref[0]) & (me % 2 == 0))
    def _():
        put(own_ref, peer_ref)

    @pl.when((me == owner_ref[0]) & (me % 2 == 1))
    def _():
        put(peer_ref, own_ref)


def place(owner, own, peer, blank):
    vmem_spec = pl.BlockSpec(memory_space=pltpu.VMEM)
    hbm_spec = pl.BlockSpec(memory_space=pltpu.HBM)
    return pl.pallas_call(
        place_kernel,
        out_shape=jax.ShapeDtypeStruct(blank.shape, BF16),
        in_specs=[pl.BlockSpec(memory_space=pltpu.SMEM), vmem_spec, vmem_spec, hbm_spec],
        out_specs=hbm_spec,
        scratch_shapes=[pltpu.VMEM(blank.shape, BF16), pltpu.SemaphoreType.DMA],
        input_output_aliases={3: 0},
        compiler_params=vmem(16),
        name="place",
    )(owner, own, peer, blank)


def per_device(queries, cache_keys, cache_values, lengths, span_owner):
    keep, send = split(queries[0])
    mine = choose(span_owner, keep, lax.ppermute(send, AXIS, SWAP))
    lengths, mine = lax.optimization_barrier((lengths, mine))
    first_keys, values, blank = turned_values(
        lengths, cache_keys, cache_values, queries.shape[1:]
    )
    y, x = span_owner[0] // (2 * COLUMNS), span_owner[0] // 2 % COLUMNS
    slot = y * COLUMNS + jnp.where(y % 2 == 1, COLUMNS - 1 - x, x)
    piece = lax.dynamic_index_in_dim(exchange(mine, PLANE), slot, 0, False)
    piece, first_keys, values = lax.optimization_barrier((piece, first_keys, values))

    own_away = exchange(jnp.broadcast_to(piece[None], (PIECES, PIECE, HEAD)), TEAMS)
    other_away = lax.ppermute(own_away, AXIS, SWAP)
    own_here = lax.ppermute(own_away, AXIS, PAIR)

    part, keys = first_attention(own_away, first_keys, cache_keys, values)
    attend = functools.partial(attention, keys=keys, values=values)
    part, other_away, own_here = lax.optimization_barrier((part, other_away, own_here))
    peer_away = lax.ppermute(part, AXIS, SWAP)
    other_here = lax.ppermute(own_here, AXIS, SWAP)
    part = attend(other_away)
    away = merge(part, peer_away)
    away, other_here = lax.optimization_barrier((away, other_here))
    here = lax.ppermute(away, AXIS, CROSS)
    part = attend(other_here)
    peer_here = lax.ppermute(part, AXIS, SWAP)
    part, own_here = lax.optimization_barrier((part, own_here))
    part = attend(own_here)

    received = exchange(merge(part, peer_here, merge(here)), TEAMS)
    result = exchange(finish(received), PLANE)
    out = place(span_owner, result, lax.ppermute(result, AXIS, SWAP), blank)
    return out[None]


def solution(mesh):
    return jax.shard_map(
        per_device,
        mesh=mesh,
        in_specs=(P("seq", None, "head"), P("seq", "head"), P("seq", "head"), P(), P()),
        out_specs=P("seq", None, "head"),
        check_vma=False,
    )
```

```python
import functools
import math

import jax
import jax.numpy as jnp
from jax import lax
from jax.experimental import pallas as pl
from jax.experimental.pallas import tpu as pltpu
from jax.sharding import PartitionSpec as P

AXIS = "seq"
CHIPS = 16
HEAD = 128
PIECE = 64
TAIL = 8
ROWS = PIECE + TAIL
VROWS = HEAD + 16
COLUMNS = 4
BLOCK = 512
PIECES = 2 * BLOCK // HEAD
STEP = 512
CHUNK = 2048
BF16 = jnp.bfloat16
F32 = jnp.float32
LOG2_SCALE = math.log2(math.e) / math.sqrt(HEAD)
NT = (((1,), (1,)), ((), ()))

SWAP = [(i, i ^ 1) for i in range(2 * CHIPS)]


def snake(chip):
    y, x = divmod(chip, COLUMNS)
    return y * COLUMNS + (COLUMNS - 1 - x if y % 2 else x)


PLANE = [[2 * snake(place) + core for place in range(CHIPS)] for core in range(2)]


def device(y, x, core):
    return (y % COLUMNS * COLUMNS + x % COLUMNS) * 2 + core


def partner(y, x, core):
    if core == 0:
        return device(y + (1 if y % 2 else -1), x, core)
    return device(y, x + (1 if x % 2 else -1), core)


EVERY = [(y, x, core) for y in range(COLUMNS) for x in range(COLUMNS) for core in range(2)]
PAIR = [(device(*place), partner(*place)) for place in EVERY]
CROSS = [(device(y, x, 1 - core), partner(y, x, core)) for y, x, core in EVERY]
def member(chip, core):
    y, x = divmod(chip, COLUMNS)
    short, long = (y, x) if core == 0 else (x, y)
    return short // 2, 2 * long + short % 2


SEATS = [
    [sorted((c for c in range(CHIPS) if member(c, core)[0] == team), key=lambda c: member(c, core)[1])
     for team in range(2)]
    for core in range(2)
]
TEAMS = [[2 * chip + core for chip in SEATS[core][team]] for core in range(2) for team in range(2)]


def vmem(limit):
    return pltpu.CompilerParams(vmem_limit_bytes=limit << 20)


def exchange(pieces, groups):
    return lax.all_to_all(pieces, AXIS, 0, 0, axis_index_groups=groups, tiled=True)


def in_hbm(array):
    return pltpu.with_memory_space_constraint(array, pltpu.HBM)


def values_kernel(len_ref, k_ref, v_ref, head_ref, o_ref, blank_ref, held_ref, zero_ref, sems):
    spans = [slice(start, start + CHUNK) for start in range(0, v_ref.shape[0], CHUNK)]
    copies = [
        pltpu.make_async_copy(v_ref.at[span], held_ref.at[span], sems.at[i])
        for i, span in enumerate(spans)
    ]
    copies.append(pltpu.make_async_copy(k_ref.at[spans[0]], head_ref, sems.at[len(spans)]))
    for copy in copies:
        copy.start()
    zero_ref[...] = jnp.zeros_like(zero_ref)
    blank = pltpu.make_async_copy(zero_ref, blank_ref, sems.at[len(spans) + 1])
    blank.start()
    lanes = lax.broadcasted_iota(jnp.int32, (HEAD, HEAD), 1)
    eye = (lanes == lax.broadcasted_iota(jnp.int32, (HEAD, HEAD), 0)).astype(BF16)
    valid_len = len_ref[lax.axis_index(AXIS)]
    for copy, span in zip(copies, spans):
        copy.wait()
        turned = lax.dot_general(eye, held_ref[span, :], NT, preferred_element_type=F32)
        valid = span.start + lax.broadcasted_iota(jnp.int32, (1, CHUNK), 1) < valid_len
        o_ref[:HEAD, span] = jnp.where(valid, turned, 0.0).astype(BF16)
        ones = jnp.broadcast_to(jnp.where(valid, 1.0, 0.0), (VROWS - HEAD, CHUNK))
        o_ref[HEAD:, span] = ones.astype(BF16)
    copies[-1].wait()
    blank.wait()


def turned_values(lengths, keys, values, shape):
    count = values.shape[0]
    hbm_spec = pl.BlockSpec(memory_space=pltpu.HBM)
    vmem_spec = pl.BlockSpec(memory_space=pltpu.VMEM)
    return pl.pallas_call(
        values_kernel,
        out_shape=(
            jax.ShapeDtypeStruct((CHUNK, HEAD), BF16),
            jax.ShapeDtypeStruct((VROWS, count), BF16),
            jax.ShapeDtypeStruct(shape, BF16),
        ),
        in_specs=[pl.BlockSpec(memory_space=pltpu.SMEM), hbm_spec, hbm_spec],
        out_specs=(vmem_spec, vmem_spec, hbm_spec),
        scratch_shapes=[
            pltpu.VMEM(values.shape, BF16),
            pltpu.VMEM(shape, BF16),
            pltpu.SemaphoreType.DMA((count // CHUNK + 2,)),
        ],
        compiler_params=vmem(16),
        cost_estimate=pl.CostEstimate(
            flops=4 * count * HEAD * HEAD, bytes_accessed=5 * count * HEAD, transcendentals=0
        ),
        name="turn_values",
    )(lengths, in_hbm(keys), in_hbm(values))


def write_block(o_ref, out, sums, top):
    row = lax.broadcasted_iota(jnp.int32, (TAIL, HEAD), 0)
    for head in range(BLOCK // HEAD):
        lanes = slice(head * HEAD, (head + 1) * HEAD)
        tail = jnp.where(row < TAIL // 2, sums[:, lanes], top[:, lanes])
        for part in range(2):
            o_ref[2 * head + part, :PIECE, :] = out[part * PIECE : (part + 1) * PIECE, lanes]
            o_ref[2 * head + part, PIECE:, :] = tail


def weigh(q, keys, values):
    scores = lax.dot_general(keys, q, NT, preferred_element_type=F32)
    weights = jnp.exp2(scores * LOG2_SCALE).astype(BF16)
    return jnp.dot(values, weights, preferred_element_type=F32)


def settle(total, q, k_ref, v_ref, o_ref, acc_ref):
    sums = total[HEAD : HEAD + 1, :]
    write_block(o_ref, total[:HEAD], sums, jnp.zeros_like(sums))
    good = (sums >= 2.0**-10) & (sums <= 2.0**20)
    bad = jnp.max(jnp.where(jnp.abs(total[:HEAD]) < 3e38, 0.0, 1.0), axis=0, keepdims=True)
    fine = jnp.max(jnp.where(good, bad, 1.0)) < 0.5

    @pl.when(jnp.logical_not(fine))
    def _():
        acc_ref[...] = jnp.zeros_like(acc_ref)
        valid_len = jnp.sum(v_ref[HEAD : HEAD + 1, :].astype(F32)).astype(jnp.int32)

        def body(i, top):
            at = pl.multiple_of(i * STEP, STEP)
            s = lax.dot_general(k_ref[pl.ds(at, STEP), :], q, NT, preferred_element_type=F32)
            row = at + lax.broadcasted_iota(jnp.int32, (STEP, 1), 0)
            s = jnp.where(row < valid_len, s * LOG2_SCALE, -jnp.inf)
            new_top = jnp.maximum(top, jnp.max(s, axis=0, keepdims=True))
            w = jnp.exp2(s - new_top).astype(BF16)
            part = jnp.dot(v_ref[:, pl.ds(at, STEP)], w, preferred_element_type=F32)
            acc_ref[...] = acc_ref[...] * jnp.exp2(top - new_top) + part
            return new_top

        start_top = jnp.full((1, BLOCK), -jnp.inf, F32)
        top = lax.fori_loop(0, k_ref.shape[0] // STEP, body, start_top)
        write_block(o_ref, acc_ref[:HEAD, :], acc_ref[HEAD : HEAD + 1, :], top)


def attention_kernel(q_ref, k_ref, v_ref, o_ref, acc_ref):
    q = q_ref[...]
    settle(weigh(q, k_ref[...], v_ref[...]), q, k_ref, v_ref, o_ref, acc_ref)


def first_attention_kernel(q_ref, head_ref, k_ref, v_ref, o_ref, kept_ref, acc_ref, sems):
    stops = [0, CHUNK, 2 * CHUNK, k_ref.shape[0]]
    spans = [slice(*ends) for ends in zip(stops, stops[1:])]
    copies = [
        pltpu.make_async_copy(k_ref.at[span] if i else head_ref, kept_ref.at[span], sems.at[i])
        for i, span in enumerate(spans)
    ]
    for copy in copies[1:] + copies[:1]:
        copy.start()
    q = q_ref[...]
    total = weigh(q, head_ref[...], v_ref[:, spans[0]])
    for copy, span in zip(copies[1:], spans[1:]):
        copy.wait()
        total += weigh(q, kept_ref[span, :], v_ref[:, span])
    copies[0].wait()
    settle(total, q, kept_ref, v_ref, o_ref, acc_ref)


def first_attention(rows, head, keys, values):
    vmem_spec = pl.BlockSpec(memory_space=pltpu.VMEM)
    return pl.pallas_call(
        first_attention_kernel,
        out_shape=(
            jax.ShapeDtypeStruct((PIECES, ROWS, HEAD), F32),
            jax.ShapeDtypeStruct(keys.shape, BF16),
        ),
        in_specs=[vmem_spec, vmem_spec, pl.BlockSpec(memory_space=pltpu.HBM), vmem_spec],
        out_specs=(vmem_spec, vmem_spec),
        scratch_shapes=[
            pltpu.VMEM((VROWS, BLOCK), F32),
            pltpu.SemaphoreType.DMA((3,)),
        ],
        compiler_params=vmem(44),
        cost_estimate=pl.CostEstimate(
            flops=BLOCK * keys.size // 2, bytes_accessed=keys.size, transcendentals=0
        ),
        name="first_attention",
    )(rows.reshape(BLOCK, HEAD), head, in_hbm(keys), values)


def attention(rows, keys, values):
    vmem_spec = pl.BlockSpec(memory_space=pltpu.VMEM)
    return pl.pallas_call(
        attention_kernel,
        out_shape=jax.ShapeDtypeStruct((PIECES, ROWS, HEAD), F32),
        in_specs=[vmem_spec] * 3,
        out_specs=vmem_spec,
        scratch_shapes=[pltpu.VMEM((VROWS, BLOCK), F32)],
        compiler_params=vmem(44),
        cost_estimate=pl.CostEstimate(
            flops=BLOCK * keys.size // 2, bytes_accessed=keys.size, transcendentals=0
        ),
        name="attention",
    )(rows.reshape(BLOCK, HEAD), keys, values)


def merge_kernel(*refs):
    parts, o_ref = refs[:-1], refs[-1]
    tops = [ref[:, ROWS - 1 :, :] for ref in parts]
    top = functools.reduce(jnp.maximum, tops)
    scales = [jnp.exp2(t - top) for t in tops]
    sums = sum(w * ref[:, PIECE : PIECE + 1, :] for w, ref in zip(scales, parts))
    row = lax.broadcasted_iota(jnp.int32, (1, TAIL, HEAD), 1)
    o_ref[:, :PIECE, :] = sum(w * ref[:, :PIECE, :] for w, ref in zip(scales, parts))
    o_ref[:, PIECE:, :] = jnp.where(row < TAIL // 2, sums, top)


def merge(*parts):
    return pl.pallas_call(
        merge_kernel,
        out_shape=jax.ShapeDtypeStruct(parts[0].shape, F32),
        compiler_params=vmem(16),
        name="merge",
    )(*parts)


def split_kernel(q_ref, keep_ref, send_ref, sems):
    half = q_ref.shape[1] // 2

    def put(ref, core, sem):
        copies = []
        for chip in range(CHIPS):
            team, place = member(chip, core)
            head, part = divmod((1 - team) * PIECES + place, 2)
            column = core * half + head * HEAD
            piece = q_ref.at[part * PIECE : (part + 1) * PIECE, column : column + HEAD]
            copies.append(pltpu.make_async_copy(piece, ref.at[snake(chip)], sem.at[chip]))
        return copies

    for core in range(2):

        @pl.when(lax.axis_index(AXIS) % 2 == core)
        def _():
            copies = put(send_ref, 1 - core, sems.at[0]) + put(keep_ref, core, sems.at[1])
            for copy in copies:
                copy.start()
            for copy in copies:
                copy.wait()


def split(block):
    shape = jax.ShapeDtypeStruct((CHIPS, PIECE, HEAD), BF16)
    vmem_spec = pl.BlockSpec(memory_space=pltpu.VMEM)
    return pl.pallas_call(
        split_kernel,
        out_shape=(shape, shape),
        in_specs=[pl.BlockSpec(memory_space=pltpu.HBM)],
        out_specs=(vmem_spec, vmem_spec),
        scratch_shapes=[pltpu.SemaphoreType.DMA((2, CHIPS))],
        compiler_params=vmem(16),
        name="split",
    )(in_hbm(block))


def choose_kernel(owner_ref, a_ref, b_ref, o_ref, sem):
    mine = owner_ref[0] % 2 == lax.axis_index(AXIS) % 2

    def put(ref):
        copy = pltpu.make_async_copy(ref, o_ref, sem)
        copy.start()
        copy.wait()

    @pl.when(mine)
    def _():
        put(a_ref)

    @pl.when(jnp.logical_not(mine))
    def _():
        put(b_ref)


def choose(owner, a, b):
    vmem_spec = pl.BlockSpec(memory_space=pltpu.VMEM)
    return pl.pallas_call(
        choose_kernel,
        out_shape=jax.ShapeDtypeStruct(a.shape, a.dtype),
        in_specs=[pl.BlockSpec(memory_space=pltpu.SMEM), vmem_spec, vmem_spec],
        out_specs=pl.BlockSpec(memory_space=pltpu.HBM),
        scratch_shapes=[pltpu.SemaphoreType.DMA],
        compiler_params=vmem(16),
        name="choose",
    )(owner, a, b)


def finish_kernel(r_ref, o_ref):
    tops = r_ref[:, ROWS - 1 :, :]
    scale = jnp.exp2(tops - jnp.max(tops, axis=0, keepdims=True))
    denom = jnp.sum(scale * r_ref[:, PIECE : PIECE + 1, :], axis=0)
    numer = jnp.sum(scale * r_ref[:, :PIECE, :], axis=0)
    result = (numer / denom).astype(BF16)
    o_ref[...] = jnp.broadcast_to(result[None], o_ref.shape)


def finish(received):
    return pl.pallas_call(
        finish_kernel,
        out_shape=jax.ShapeDtypeStruct((CHIPS, PIECE, HEAD), BF16),
        compiler_params=vmem(16),
        name="finish",
    )(received)


def place_kernel(owner_ref, own_ref, peer_ref, blank_ref, o_ref, held_ref, sem):
    half = held_ref.shape[1] // 2
    me = lax.axis_index(AXIS)

    def put(*halves):
        for core, ref in enumerate(halves):
            for team in range(2):
                chips = SEATS[core][team]
                for spot in range(0, PIECES, 2):
                    pieces = [ref[snake(chip)] for chip in chips[spot : spot + 2]]
                    column = core * half + (team * PIECES + spot) // 2 * HEAD
                    held_ref[:, column : column + HEAD] = jnp.concatenate(pieces, axis=0).T
        copy = pltpu.make_async_copy(held_ref, o_ref, sem)
        copy.start()
        copy.wait()

    @pl.when((me == owner_ref[0]) & (me % 2 == 0))
    def _():
        put(own_ref, peer_ref)

    @pl.when((me == owner_ref[0]) & (me % 2 == 1))
    def _():
        put(peer_ref, own_ref)


def place(owner, own, peer, blank):
    vmem_spec = pl.BlockSpec(memory_space=pltpu.VMEM)
    hbm_spec = pl.BlockSpec(memory_space=pltpu.HBM)
    return pl.pallas_call(
        place_kernel,
        out_shape=jax.ShapeDtypeStruct(blank.shape, BF16),
        in_specs=[pl.BlockSpec(memory_space=pltpu.SMEM), vmem_spec, vmem_spec, hbm_spec],
        out_specs=hbm_spec,
        scratch_shapes=[pltpu.VMEM(blank.shape, BF16), pltpu.SemaphoreType.DMA],
        input_output_aliases={3: 0},
        compiler_params=vmem(16),
        name="place",
    )(owner, own, peer, blank)


def per_device(queries, cache_keys, cache_values, lengths, span_owner):
    keep, send = split(queries[0])
    mine = choose(span_owner, keep, lax.ppermute(send, AXIS, SWAP))
    lengths, mine = lax.optimization_barrier((lengths, mine))
    first_keys, values, blank = turned_values(
        lengths, cache_keys, cache_values, queries.shape[1:]
    )
    y, x = span_owner[0] // (2 * COLUMNS), span_owner[0] // 2 % COLUMNS
    slot = y * COLUMNS + jnp.where(y % 2 == 1, COLUMNS - 1 - x, x)
    piece = lax.dynamic_index_in_dim(exchange(mine, PLANE), slot, 0, False)
    piece, first_keys, values = lax.optimization_barrier((piece, first_keys, values))

    own_away = exchange(jnp.broadcast_to(piece[None], (PIECES, PIECE, HEAD)), TEAMS)
    other_away = lax.ppermute(own_away, AXIS, SWAP)
    own_here = lax.ppermute(own_away, AXIS, PAIR)

    part, keys = first_attention(own_away, first_keys, cache_keys, values)
    attend = functools.partial(attention, keys=keys, values=values)
    part, other_away, own_here = lax.optimization_barrier((part, other_away, own_here))
    peer_away = lax.ppermute(part, AXIS, SWAP)
    other_here = lax.ppermute(own_here, AXIS, SWAP)
    part = attend(other_away)
    away = merge(part, peer_away)
    away, other_here = lax.optimization_barrier((away, other_here))
    here = lax.ppermute(away, AXIS, CROSS)
    part = attend(other_here)
    peer_here = lax.ppermute(part, AXIS, SWAP)
    part, own_here = lax.optimization_barrier((part, own_here))
    part = attend(own_here)

    received = exchange(merge(part, peer_here, merge(here)), TEAMS)
    result = exchange(finish(received), PLANE)
    out = place(span_owner, result, lax.ppermute(result, AXIS, SWAP), blank)
    return out[None]


def solution(mesh):
    return jax.shard_map(
        per_device,
        mesh=mesh,
        in_specs=(P("seq", None, "head"), P("seq", "head"), P("seq", "head"), P(), P()),
        out_specs=P("seq", None, "head"),
        check_vma=False,
    )
```
